512 devices in a mesh: fsdp: 64 (over x_lo, z, core), sp: 8 (over y, x_hi).
Axes of the slice: x: 4 (x_hi: 2, x_lo: 2; x = x_hi * 2 + x_lo), y: 4, z: 16, core: 2. Of those that a mesh axis runs over, the one named last changes fastest.
Arguments:
- qkv_txt: bfloat16 [64, 3, 256, 2048], P('fsdp', None, 'sp'), may hold values from -5 to 5
- qkv_img: bfloat16 [64, 3, 768, 2048], P('fsdp', None, 'sp'), may hold values from -5 to 5
- dy_txt: bfloat16 [64, 256, 3072], P('fsdp', 'sp'), may hold values from -6 to 6
- dy_img: bfloat16 [64, 768, 3072], P('fsdp', 'sp'), may hold values from -16 to 16
- wv_txt: bfloat16 [3072, 2048], P('fsdp', 'sp'), may hold values from -0.109375 to 0.109375
- sc_txt: float32 [3072, 16], P('fsdp', 'sp'), may hold values from 0.5 to 2
- wv_img: bfloat16 [3072, 2048], P('fsdp', 'sp'), may hold values from -0.109375 to 0.109375
- sc_img: float32 [3072, 16], P('fsdp', 'sp'), may hold values from 0.5 to 2
Outputs:
- grad_qkv_txt: bfloat16 [64, 3, 256, 2048], P('fsdp', None, 'sp')
- grad_qkv_img: bfloat16 [64, 3, 768, 2048], P('fsdp', None, 'sp')
- grad_w_img: float32 [3072, 2048], P('fsdp', 'sp')
The draws below stay inside these ranges and needn't reach their ends.
All inputs are finite; a program needn't handle non-finite values.
Results may differ from the reference program's by a relative error of at most 0.02.
Values may be sent and summed in bfloat16 or wider, within the bound.
No kernel may reach another device: no remote copies, remote signals or barrier semaphores. Data moves between devices by JAX's collectives and lax.ppermute only.
A program may use at most 64 MiB of HBM per device.

```python
import math
import jax
import jax.numpy as jnp
from jax import lax

D = 3072
HEADS = 16
HD = 128
TXT = 256
IMG = 768
F = 2048
SAMPLES = 64


def draw_qkv_txt(key, part):
    key = jax.random.fold_in(key, 3)
    width = HEADS * HD
    shape = (SAMPLES, 3, TXT, width)
    first = jax.random.fold_in(key, 0)
    return jnp.clip(jax.random.normal(first, shape, jnp.float32), -4.5, 4.5).astype(jnp.bfloat16)


def draw_qkv_img(key, part):
    key = jax.random.fold_in(key, 11)
    width = HEADS * HD
    shape = (SAMPLES, 3, IMG, width)
    first = jax.random.fold_in(key, 0)
    return jnp.clip(jax.random.normal(first, shape, jnp.float32), -4.5, 4.5).astype(jnp.bfloat16)


def with_spikes(drawn, own_key, source, target, parts, factor):
    owner, partner = [(jnp.arange(drawn.shape[position]) // (drawn.shape[position] // parts)).reshape([-1 if axis == position else 1 for axis in range(drawn.ndim)]) for position in (source, target)]
    chosen = jax.random.permutation(own_key, parts)[partner]
    strong = (owner == chosen) | (owner == (partner + parts // 2) % parts)
    return jnp.where(strong, factor * drawn, drawn)


def block_scale(stream_key, extent, cuts, low, top_value):
    def one(dim, parts):
        draws = jax.random.uniform(jax.random.fold_in(jax.random.fold_in(stream_key, 6), dim), (parts,), jnp.float32, low / len(cuts), top_value / len(cuts))
        return jnp.repeat(jnp.exp(draws), extent[dim] // parts).reshape((-1,) + (1,) * (len(extent) - dim - 1))

    factor_of = one(*cuts[0])
    for cut in cuts[1:]:
        factor_of = factor_of * one(*cut)
    return factor_of


def scatter_about(stream_key, extent, scale, bound, pieces=(), held_as=jnp.bfloat16):
    entries = scale * jax.random.normal(stream_key, extent, jnp.float32)
    if pieces:
        entries = entries * block_scale(stream_key, extent, pieces, -0.22, 0.18)
    return jnp.clip(entries, -bound, bound).astype(held_as)


def noise_with(own_key, dims, scale, reach, cuts, heavy, dtype=jnp.bfloat16):
    entries = scale * jax.random.normal(own_key, dims, jnp.float32)
    if cuts:
        entries = entries * block_scale(own_key, dims, cuts, -0.22, 0.18)
    return jnp.clip(with_spikes(entries, jax.random.fold_in(own_key, 3), *heavy), -reach, reach).astype(dtype)


def setup_inputs(seed: int = 0) -> dict:
    key_of = jax.random.split(jax.random.key(seed), 9)
    return {
        "qkv_txt": draw_qkv_txt(jax.random.fold_in(key_of[8], 71), 0),
        "qkv_img": draw_qkv_img(jax.random.fold_in(key_of[8], 71), 0),
        "dy_txt": scatter_about(key_of[2], (SAMPLES, TXT, D), 1.0, 6.0, ((0, 64), (1, 8))),
        "dy_img": noise_with(key_of[3], (SAMPLES, IMG, D), 1.0, 16.0, ((0, 64), (1, 8)), (0, 2, 64, 4.0)),
        "wv_txt": scatter_about(key_of[4], (D, F), D ** -0.5, 0.109375, ((0, 64), (1, 8))),
        "sc_txt": jnp.clip(jnp.exp(math.log(2.0) - 1.3862944 * jax.random.uniform(key_of[5], (D, HEADS), jnp.float32) ** block_scale(key_of[5], (D, HEADS), ((0, 64), (1, 8)), -0.2, 0.2)), 0.5, 2.0),
        "wv_img": scatter_about(key_of[6], (D, F), D ** -0.5, 0.109375, ((0, 64), (1, 8))),
        "sc_img": jnp.clip(jnp.exp(math.log(2.0) - 1.3862944 * jax.random.uniform(key_of[7], (D, HEADS), jnp.float32) ** block_scale(key_of[7], (D, HEADS), ((0, 64), (1, 8)), -0.2, 0.2)), 0.5, 2.0),
    }


def dequant(values, scales):
    return (values.astype(jnp.float32) * jnp.repeat(scales, HD, axis=1)).astype(jnp.bfloat16)

def rounded(tensor):
    return lax.optimization_barrier(tensor.astype(jnp.bfloat16)).astype(jnp.float32)

def reference(qkv_txt, qkv_img, dy_txt, dy_img, wv_txt, sc_txt, wv_img, sc_img):
    w_txt = dequant(wv_txt, sc_txt)
    w_img = dequant(wv_img, sc_img)
    factor = 1.0 / math.sqrt(HD)

    def one_sample(total, item):
        text_part, image_part, upstream_txt, upstream_img = item
        joint = jnp.concatenate([text_part, image_part], axis=1)
        length = joint.shape[1]
        grad_out = jnp.concatenate([jnp.dot(upstream_txt, w_txt, preferred_element_type=jnp.float32), jnp.dot(upstream_img, w_img, preferred_element_type=jnp.float32)], axis=0).astype(jnp.bfloat16)
        queries = joint[0].reshape(length, HEADS, HD).astype(jnp.float32)
        keyset = joint[1].reshape(length, HEADS, HD).astype(jnp.float32)
        valueset = joint[2].reshape(length, HEADS, HD).astype(jnp.float32)
        scores = jnp.einsum('qhd,khd->hqk', queries, keyset) * factor
        probs = jax.nn.softmax(scores, axis=-1)
        probs_low = rounded(probs)
        attended = rounded(jnp.einsum('hqk,khd->qhd', probs_low, valueset))
        grad_heads = grad_out.reshape(length, HEADS, HD).astype(jnp.float32)
        delta = lax.optimization_barrier(jnp.sum(grad_heads * attended, axis=-1))
        prob_grad = jnp.einsum('qhd,khd->hqk', grad_heads, valueset)
        score_grad = rounded(probs * (prob_grad - delta.T[:, :, None]))
        grad_query = jnp.einsum('hqk,khd->qhd', score_grad, keyset) * factor
        grad_keys = jnp.einsum('hqk,qhd->khd', score_grad, queries) * factor
        grad_values = jnp.einsum('hqk,qhd->khd', probs_low, grad_heads)
        grads = jnp.stack([grad_query, grad_keys, grad_values]).reshape(3, length, HEADS * HD).astype(jnp.bfloat16)
        image_attended = attended[TXT:].reshape(IMG, HEADS * HD).astype(jnp.bfloat16)
        term = lax.dot_general(upstream_img, image_attended, (((0,), (0,)), ((), ())), preferred_element_type=jnp.float32)
        return (total + term, (grads[:, :TXT], grads[:, TXT:]))
    start = jnp.zeros((D, HEADS * HD), jnp.float32)
    total, (grad_txt, grad_img) = lax.scan(one_sample, start, (qkv_txt, qkv_img, dy_txt, dy_img))
    return (grad_txt, grad_img, total / SAMPLES)
```

```python
import functools
import math

import jax
import jax.numpy as jnp
from jax import lax
from jax.experimental import pallas as pl
from jax.experimental.pallas import tpu as pltpu
from jax.sharding import PartitionSpec as P

HD = 128
SP = 8
TXT = 32
IMG = 96
TOK = TXT + IMG
ALL_TXT = SP * TXT
LENGTH = SP * TOK
COLS = 256
D = 3072
ROWS = 48
HEADS = COLS // HD
CHUNK = 256
FACTOR = 1.0 / math.sqrt(HD)
LOG2E = 1.4426950408889634
SCALE2 = FACTOR * LOG2E
AXES = ("fsdp", "sp")
VMEM_LIMIT = 48 * 1024 * 1024


def number(x_lo, z, core, y, x_hi):
    return ((x_lo * 16 + z) * 2 + core) * SP + y * 2 + x_hi


def every():
    return [
        (x_lo, z, core, y, x_hi)
        for x_lo in range(2)
        for z in range(16)
        for core in range(2)
        for y in range(4)
        for x_hi in range(2)
    ]


def route(target):
    return [(number(*d), number(*target(*d))) for d in every()]


SWAP_CORE = route(lambda x_lo, z, core, y, x_hi: (x_lo, z, 1 - core, y, x_hi))
SWAP_X_LO = route(lambda x_lo, z, core, y, x_hi: (1 - x_lo, z, core, y, x_hi))
SWAP_X_HI = route(lambda x_lo, z, core, y, x_hi: (x_lo, z, core, y, 1 - x_hi))
FROM_Y = {
    k: route(lambda x_lo, z, core, y, x_hi, k=k: (x_lo, z, core, (y - k) % 4, x_hi))
    for k in (1, 2, 3)
}
Z_GROUPS = [
    [number(x_lo, z, core, y, x_hi) for z in range(16)]
    for x_lo in range(2)
    for core in range(2)
    for y in range(4)
    for x_hi in range(2)
]


def send(x, pairs):
    return lax.ppermute(x, AXES, pairs)


def dequant(values, scales):
    return (values.astype(jnp.float32) * jnp.repeat(scales, HD, axis=1)).astype(jnp.bfloat16)


def dot(a, b):
    return jnp.dot(a, b, preferred_element_type=jnp.float32)


def dot_last(a, b):
    return lax.dot_general(a, b, (((1,), (1,)), ((), ())), preferred_element_type=jnp.float32)


def transposed(x):
    return x.astype(jnp.float32).T


def load_qkv(x_ref, joint, sems):
    copies = []
    for r in range(SP):
        copies.append(
            pltpu.make_async_copy(
                x_ref.at[r, :, pl.ds(0, TXT), :],
                joint.at[:, pl.ds(r * TXT, TXT), :],
                sems.at[2 * r],
            )
        )
        copies.append(
            pltpu.make_async_copy(
                x_ref.at[r, :, pl.ds(TXT, IMG), :],
                joint.at[:, pl.ds(ALL_TXT + r * IMG, IMG), :],
                sems.at[2 * r + 1],
            )
        )
    for copy in copies:
        copy.start()
    return copies


def forward_kernel(x_ref, att_ref, lse_ref, joint, sems):
    for copy in load_qkv(x_ref, joint, sems):
        copy.wait()
    for head in range(HEADS):
        window = slice(head * HD, (head + 1) * HD)
        keys = joint[1, :, window]
        values_t = transposed(joint[2, :, window]).astype(jnp.bfloat16)
        for chunk in range(LENGTH // CHUNK):
            rows = slice(chunk * CHUNK, (chunk + 1) * CHUNK)
            scores = dot_last(keys, joint[0, rows, window])
            highest = jnp.max(scores, axis=0, keepdims=True)
            weights = jnp.exp2((scores - highest) * SCALE2)
            total = jnp.sum(weights, axis=0, keepdims=True)
            att_t = dot(values_t, weights.astype(jnp.bfloat16)) / total
            att_ref[rows, window] = att_t.T.astype(jnp.bfloat16)
            lse_ref[head : head + 1, rows] = highest * SCALE2 + jnp.log2(total)


def forward(x):
    return pl.pallas_call(
        forward_kernel,
        out_shape=(
            jax.ShapeDtypeStruct((LENGTH, COLS), jnp.bfloat16),
            jax.ShapeDtypeStruct((HEADS, LENGTH), jnp.float32),
        ),
        in_specs=[pl.BlockSpec(memory_space=pl.ANY)],
        out_specs=(
            pl.BlockSpec(memory_space=pltpu.VMEM),
            pl.BlockSpec(memory_space=pltpu.VMEM),
        ),
        scratch_shapes=[
            pltpu.VMEM((3, LENGTH, COLS), jnp.bfloat16),
            pltpu.SemaphoreType.DMA((2 * SP,)),
        ],
        compiler_params=pltpu.CompilerParams(vmem_limit_bytes=VMEM_LIMIT),
        cost_estimate=pl.CostEstimate(
            flops=HEADS * 4 * LENGTH * LENGTH * HD,
            bytes_accessed=4 * LENGTH * COLS * 2,
            transcendentals=HEADS * LENGTH * LENGTH,
        ),
        name="attention_forward",
    )(x)


def slots(sp):
    y, x_hi = sp // 2, sp % 2
    return [((y + k) % 4) * 2 + x_hi for k in range(4)] + [
        ((y + k) % 4) * 2 + 1 - x_hi for k in range(4)
    ]


def load_dy(place_ref, pieces, text, image, sems):
    copies = []
    for n, piece in enumerate(pieces):
        slot = place_ref[n]
        if text is not None:
            copies.append(
                pltpu.make_async_copy(
                    piece.at[pl.ds(0, TXT), :],
                    text.at[pl.ds(pl.multiple_of(slot * TXT, TXT), TXT), :],
                    sems.at[2 * n],
                )
            )
        copies.append(
            pltpu.make_async_copy(
                piece.at[pl.ds(TXT, IMG), :],
                image.at[pl.ds(pl.multiple_of(slot * IMG, TXT), IMG), :],
                sems.at[2 * n + 1],
            )
        )
    for copy in copies:
        copy.start()
    return copies


BAND = 8 * 2 * ROWS


def term_kernel(place_ref, *refs):
    pieces, (att_ref, keep_ref, give_ref, image, sems) = refs[:SP], refs[SP:]
    copies = load_dy(place_ref, pieces, None, image, sems)
    att_t = transposed(att_ref[ALL_TXT:, :]).astype(jnp.bfloat16)
    for copy in copies:
        copy.wait()
    core, x_lo = place_ref[SP], place_ref[SP + 1]
    for band in range(D // BAND):
        term = dot(att_t, image[:, band * BAND : (band + 1) * BAND]).T.astype(jnp.bfloat16)
        far = (x_lo + band // 2) % 2
        for j in range(8):
            z = (band % 2) * 8 + j
            low = term[(2 * j) * ROWS : (2 * j + 1) * ROWS]
            high = term[(2 * j + 1) * ROWS : (2 * j + 2) * ROWS]
            keep_ref[far, z] = jnp.where(core == 0, low, high)
            give_ref[far, z] = jnp.where(core == 0, high, low)


def weight_term(place, pieces, att):
    half = jax.ShapeDtypeStruct((2, 16, ROWS, COLS), jnp.bfloat16)
    return pl.pallas_call(
        term_kernel,
        out_shape=(half, half),
        in_specs=[pl.BlockSpec(memory_space=pltpu.SMEM)]
        + [pl.BlockSpec(memory_space=pl.ANY)] * SP
        + [pl.BlockSpec(memory_space=pltpu.VMEM)],
        out_specs=(
            pl.BlockSpec(memory_space=pltpu.VMEM),
            pl.BlockSpec(memory_space=pltpu.VMEM),
        ),
        scratch_shapes=[
            pltpu.VMEM((SP * IMG, D), jnp.bfloat16),
            pltpu.SemaphoreType.DMA((2 * SP,)),
        ],
        compiler_params=pltpu.CompilerParams(vmem_limit_bytes=VMEM_LIMIT),
        cost_estimate=pl.CostEstimate(
            flops=2 * SP * IMG * D * COLS,
            bytes_accessed=SP * IMG * D * 2 + D * COLS * 2,
            transcendentals=0,
        ),
        name="weight_term",
    )(place, *pieces, att)


def head_backward(head, joint, grad, att, lse, probs, slopes, out_ref):
    window = slice(head * HD, (head + 1) * HD)
    keys, values = joint[1, :, window], joint[2, :, window]
    keys_t = transposed(keys).astype(jnp.bfloat16)

    def put(member, first, block):
        for r in range(SP):
            lo, hi = r * TXT - first, (r + 1) * TXT - first
            if 0 <= lo < block.shape[0]:
                out_ref[r, member, :TXT, :] = block[lo:hi]
            lo, hi = ALL_TXT + r * IMG - first, ALL_TXT + (r + 1) * IMG - first
            start, stop = max(lo, 0), min(hi, block.shape[0])
            if start < stop:
                out_ref[r, member, TXT + start - lo : TXT + stop - lo, :] = block[start:stop]

    for chunk in range(LENGTH // CHUNK):
        rows = slice(chunk * CHUNK, (chunk + 1) * CHUNK)
        out_grad = grad[rows, window]
        product = out_grad.astype(jnp.float32) * att[rows, window].astype(jnp.float32)
        delta = jnp.sum(product.T, axis=0, keepdims=True)
        scores = dot_last(keys, joint[0, rows, window])
        weights = jnp.exp2(scores * SCALE2 - lse[head : head + 1, rows])
        probs[:, rows] = weights.astype(jnp.bfloat16)
        slope = (weights * (dot_last(values, out_grad) - delta)).astype(jnp.bfloat16)
        slopes[:, rows] = slope
        grad_query = (dot(keys_t, slope) * FACTOR).T.astype(jnp.bfloat16)
        put(0, chunk * CHUNK, grad_query)
    put(1, 0, (dot(slopes[...], joint[0, :, window]) * FACTOR).astype(jnp.bfloat16))
    put(2, 0, dot(probs[...], grad[:, window]).astype(jnp.bfloat16))


def first_kernel(place_ref, *refs):
    pieces, rest = refs[:SP], refs[SP:]
    w_ref, x_ref, att, lse, out_ref, grad, text, image, weight, joint, probs, slopes = rest[:12]
    dy_sems, qkv_sems, w_sems = rest[12:]
    copies = [
        pltpu.make_async_copy(
            w_ref.at[:, x_lo, :, stream], weight.at[stream, x_lo], w_sems.at[2 * stream + x_lo]
        )
        for stream in range(2)
        for x_lo in range(2)
    ]
    for copy in copies:
        copy.start()
    copies += load_dy(place_ref, pieces, text, image, dy_sems)
    copies += load_qkv(x_ref, joint, qkv_sems)
    for copy in copies:
        copy.wait()
    grad[:ALL_TXT, :] = dot(text[...], weight[0].reshape(D, COLS)).astype(jnp.bfloat16)
    grad[ALL_TXT:, :] = dot(image[...], weight[1].reshape(D, COLS)).astype(jnp.bfloat16)
    head_backward(0, joint, grad, att, lse, probs, slopes, out_ref)


def second_kernel(x_ref, grad, att, lse, out_ref, joint, probs, slopes, qkv_sems):
    for copy in load_qkv(x_ref, joint, qkv_sems):
        copy.wait()
    head_backward(1, joint, grad, att, lse, probs, slopes, out_ref)


ANY = pl.BlockSpec(memory_space=pl.ANY)
VMEM = pl.BlockSpec(memory_space=pltpu.VMEM)
BLOCKS = jax.ShapeDtypeStruct((SP, 3, TOK, HD), jnp.bfloat16)
JOINT = pltpu.VMEM((3, LENGTH, COLS), jnp.bfloat16)
SQUARE = pltpu.VMEM((LENGTH, LENGTH), jnp.bfloat16)
BACK_FLOPS = 10 * LENGTH * LENGTH * HD


def backward_first(place, pieces, w, x, att, lse):
    return pl.pallas_call(
        first_kernel,
        out_shape=(BLOCKS, jax.ShapeDtypeStruct((LENGTH, COLS), jnp.bfloat16)),
        in_specs=[pl.BlockSpec(memory_space=pltpu.SMEM)] + [ANY] * (SP + 2) + [VMEM] * 2,
        out_specs=(VMEM, VMEM),
        scratch_shapes=[
            pltpu.VMEM((ALL_TXT, D), jnp.bfloat16),
            pltpu.VMEM((SP * IMG, D), jnp.bfloat16),
            pltpu.VMEM((2, 2, 16, 2, ROWS, COLS), jnp.bfloat16),
            JOINT,
            SQUARE,
            SQUARE,
            pltpu.SemaphoreType.DMA((2 * SP,)),
            pltpu.SemaphoreType.DMA((2 * SP,)),
            pltpu.SemaphoreType.DMA((4,)),
        ],
        compiler_params=pltpu.CompilerParams(vmem_limit_bytes=VMEM_LIMIT),
        cost_estimate=pl.CostEstimate(
            flops=BACK_FLOPS + 2 * LENGTH * D * COLS,
            bytes_accessed=LENGTH * D * 2 + 2 * D * COLS * 2 + 5 * LENGTH * COLS * 2,
            transcendentals=LENGTH * LENGTH,
        ),
        name="backward_first_head",
    )(place, *pieces, w, x, att, lse)


def backward_second(x, grad, att, lse):
    return pl.pallas_call(
        second_kernel,
        out_shape=BLOCKS,
        in_specs=[ANY] + [VMEM] * 3,
        out_specs=VMEM,
        scratch_shapes=[JOINT, SQUARE, SQUARE, pltpu.SemaphoreType.DMA((2 * SP,))],
        compiler_params=pltpu.CompilerParams(vmem_limit_bytes=VMEM_LIMIT),
        cost_estimate=pl.CostEstimate(
            flops=BACK_FLOPS,
            bytes_accessed=6 * LENGTH * COLS * 2,
            transcendentals=LENGTH * LENGTH,
        ),
        name="backward_second_head",
    )(x, grad, att, lse)


def gather_weights(wv_txt, sc_txt, wv_img, sc_img, core, x_lo):
    own = jnp.stack([dequant(wv_txt, sc_txt), dequant(wv_img, sc_img)])
    other = send(own, SWAP_CORE)
    pair = jnp.where(core == 0, jnp.stack([own, other]), jnp.stack([other, own]))
    other = send(pair, SWAP_X_LO)
    four = jnp.where(x_lo == 0, jnp.stack([pair, other]), jnp.stack([other, pair]))
    return lax.all_gather(four, AXES, axis=0, axis_index_groups=Z_GROUPS)


def sum_over_samples(keep, give):
    near = keep.astype(jnp.float32) + send(give, SWAP_CORE).astype(jnp.float32)
    far = send(near[1].astype(jnp.bfloat16), SWAP_X_LO)
    four = (near[0] + far.astype(jnp.float32)).astype(jnp.bfloat16)
    parts = lax.all_to_all(four, AXES, 0, 0, axis_index_groups=Z_GROUPS, tiled=True)
    return jnp.sum(parts.astype(jnp.float32), axis=0) * (1.0 / 64)


def local(qkv_txt, qkv_img, dy_txt, dy_img, wv_txt, sc_txt, wv_img, sc_img):
    fsdp, sp = lax.axis_index("fsdp"), lax.axis_index("sp")
    core, x_lo = fsdp % 2, fsdp // 32
    place = jnp.stack(slots(sp) + [core, x_lo]).astype(jnp.int32)

    w = gather_weights(wv_txt, sc_txt, wv_img, sc_img, core, x_lo)

    own = jnp.concatenate([dy_txt[0], dy_img[0]], axis=0)
    other = send(own, SWAP_X_HI)
    pieces = (
        [own]
        + [send(own, FROM_Y[k]) for k in (1, 2, 3)]
        + [other]
        + [send(other, FROM_Y[k]) for k in (1, 2, 3)]
    )

    x = jnp.concatenate(
        [qkv_txt[0].reshape(3, TXT, SP, COLS), qkv_img[0].reshape(3, IMG, SP, COLS)], axis=1
    ).transpose(2, 0, 1, 3)
    x = lax.all_to_all(x, "sp", 0, 0, tiled=True)

    att, lse = forward(x)
    keep, give = weight_term(place, pieces, att)
    weight_grad = sum_over_samples(keep, give)

    first, grad = backward_first(place, pieces, w, x, att, lse)
    second = backward_second(x, grad, att, lse)
    back = jnp.stack(
        [lax.all_to_all(part, "sp", 0, 0, tiled=True) for part in (first, second)], axis=3
    )
    back = back.transpose(1, 2, 0, 3, 4).reshape(1, 3, TOK, SP * COLS)
    return (back[:, :, :TXT], back[:, :, TXT:], weight_grad)


def solution(mesh):
    placed = (
        P("fsdp", None, "sp", None),
        P("fsdp", None, "sp", None),
        P("fsdp", "sp", None),
        P("fsdp", "sp", None),
        P("fsdp", "sp"),
        P("fsdp", "sp"),
        P("fsdp", "sp"),
        P("fsdp", "sp"),
    )
    return jax.shard_map(
        local,
        mesh=mesh,
        in_specs=placed,
        out_specs=(P("fsdp", None, "sp", None), P("fsdp", None, "sp", None), P("fsdp", "sp")),
        check_vma=False,
    )
```

```python
import functools
import math

import jax
import jax.numpy as jnp
from jax import lax
from jax.experimental import pallas as pl
from jax.experimental.pallas import tpu as pltpu
from jax.sharding import PartitionSpec as P

HD = 128
SP = 8
TXT = 32
IMG = 96
TOK = TXT + IMG
ALL_TXT = SP * TXT
ALL_IMG = SP * IMG
LENGTH = SP * TOK
COLS = 256
D = 3072
ROWS = 48
HEADS = COLS // HD
CHUNK = 256
FACTOR = 1.0 / math.sqrt(HD)
LOG2E = 1.4426950408889634
SCALE2 = FACTOR * LOG2E
AXES = ("fsdp", "sp")
VMEM_LIMIT = 48 * 1024 * 1024
LIGHT = pl.CostEstimate(flops=1000, bytes_accessed=1000, transcendentals=0)


def number(x_lo, z, core, y, x_hi):
    return ((x_lo * 16 + z) * 2 + core) * SP + y * 2 + x_hi


def every():
    return [
        (x_lo, z, core, y, x_hi)
        for x_lo in range(2)
        for z in range(16)
        for core in range(2)
        for y in range(4)
        for x_hi in range(2)
    ]


def route(target):
    return [(number(*d), number(*target(*d))) for d in every()]


SWAP_CORE = route(lambda x_lo, z, core, y, x_hi: (x_lo, z, 1 - core, y, x_hi))
SWAP_X_LO = route(lambda x_lo, z, core, y, x_hi: (1 - x_lo, z, core, y, x_hi))
SWAP_X_HI = route(lambda x_lo, z, core, y, x_hi: (x_lo, z, core, y, 1 - x_hi))
FROM_Y = {
    k: route(lambda x_lo, z, core, y, x_hi, k=k: (x_lo, z, core, (y - k) % 4, x_hi))
    for k in (1, 2, 3)
}
TO_Z = {
    k: route(lambda x_lo, z, core, y, x_hi, d=d: (x_lo, (z + d) % 16, core, y, x_hi))
    for k, d in ((4, 4), (8, 8), (12, -4))
}
Z_NEAR_GROUPS = [
    [number(x_lo, 4 * quad + z, core, y, x_hi) for z in range(4)]
    for x_lo in range(2)
    for quad in range(4)
    for core in range(2)
    for y in range(4)
    for x_hi in range(2)
]
Z_CORE_GROUPS = [
    [number(x_lo, z, core, y, x_hi) for z in range(16) for core in range(2)]
    for x_lo in range(2)
    for y in range(4)
    for x_hi in range(2)
]


def send(x, pairs):
    return lax.ppermute(x, AXES, pairs)


def dequant(values, scales):
    return (values.astype(jnp.float32) * jnp.repeat(scales, HD, axis=1)).astype(jnp.bfloat16)


def plus(a, b):
    return a.astype(jnp.float32) + b.astype(jnp.float32)


def dot(a, b):
    return jnp.dot(a, b, preferred_element_type=jnp.float32)


def dot_last(a, b):
    return lax.dot_general(a, b, (((1,), (1,)), ((), ())), preferred_element_type=jnp.float32)


def transposed(x):
    return x.astype(jnp.float32).T


def load_qkv(x_ref, joint, sems):
    copies = []
    for r in range(SP):
        copies.append(
            pltpu.make_async_copy(
                x_ref.at[r, :, pl.ds(0, TXT), :],
                joint.at[:, pl.ds(r * TXT, TXT), :],
                sems.at[2 * r],
            )
        )
        copies.append(
            pltpu.make_async_copy(
                x_ref.at[r, :, pl.ds(TXT, IMG), :],
                joint.at[:, pl.ds(ALL_TXT + r * IMG, IMG), :],
                sems.at[2 * r + 1],
            )
        )
    for copy in copies:
        copy.start()
    return copies


def forward_kernel(x_ref, att_ref, probs_ref, joint, sems):
    for copy in load_qkv(x_ref, joint, sems):
        copy.wait()
    for head in range(HEADS):
        window = slice(head * HD, (head + 1) * HD)
        keys = joint[1, :, window]
        values_t = transposed(joint[2, :, window]).astype(jnp.bfloat16)
        for chunk in range(LENGTH // CHUNK):
            rows = slice(chunk * CHUNK, (chunk + 1) * CHUNK)
            scores = dot_last(keys, joint[0, rows, window])
            highest = jnp.max(scores, axis=0, keepdims=True)
            weights = jnp.exp2((scores - highest) * SCALE2)
            share = 1.0 / jnp.sum(weights, axis=0, keepdims=True)
            probs = (weights * share).astype(jnp.bfloat16)
            probs_ref[head, :, rows] = probs
            att_ref[rows, window] = dot(values_t, probs).T.astype(jnp.bfloat16)


def forward(x):
    return pl.pallas_call(
        forward_kernel,
        out_shape=(
            jax.ShapeDtypeStruct((LENGTH, COLS), jnp.bfloat16),
            jax.ShapeDtypeStruct((HEADS, LENGTH, LENGTH), jnp.bfloat16),
        ),
        in_specs=[pl.BlockSpec(memory_space=pl.ANY)],
        out_specs=(
            pl.BlockSpec(memory_space=pltpu.VMEM),
            pl.BlockSpec(memory_space=pltpu.VMEM),
        ),
        scratch_shapes=[
            pltpu.VMEM((3, LENGTH, COLS), jnp.bfloat16),
            pltpu.SemaphoreType.DMA((2 * SP,)),
        ],
        compiler_params=pltpu.CompilerParams(vmem_limit_bytes=VMEM_LIMIT),
        cost_estimate=LIGHT,
        name="attention_forward",
    )(x)


def slots(sp):
    y, x_hi = sp // 2, sp % 2
    return [((y + k) % 4) * 2 + x_hi for k in range(4)] + [
        ((y + k) % 4) * 2 + 1 - x_hi for k in range(4)
    ]


def load_dy(place_ref, pieces, text, image, sems):
    copies = []
    parts = [(image, TXT, IMG)] + ([(text, 0, TXT)] if text is not None else [])
    for part, (target, row, size) in enumerate(parts):
        for n, piece in enumerate(pieces):
            first = pl.multiple_of(place_ref[n] * size, TXT)
            copies.append(
                pltpu.make_async_copy(
                    piece.at[pl.ds(row, size), :],
                    target.at[pl.ds(first, size), :],
                    sems.at[part * SP + n],
                )
            )
    for copy in copies:
        copy.start()
    return copies


BAND = 8 * 2 * ROWS


def term_kernel(place_ref, *refs):
    pieces, (att_ref, keep_ref, give_ref, image, sems) = refs[:SP], refs[SP:]
    copies = load_dy(place_ref, pieces, None, image, sems)
    att_t = transposed(att_ref[ALL_TXT:, :]).astype(jnp.bfloat16)
    for copy in copies:
        copy.wait()
    core, x_lo = place_ref[SP], place_ref[SP + 1]
    for band in range(D // BAND):
        term = dot(att_t, image[:, band * BAND : (band + 1) * BAND]).T.astype(jnp.bfloat16)
        far = (x_lo + band // 2) % 2
        for j in range(8):
            z = (band % 2) * 8 + j
            low = term[(2 * j) * ROWS : (2 * j + 1) * ROWS]
            high = term[(2 * j + 1) * ROWS : (2 * j + 2) * ROWS]
            keep_ref[far, z % 4, z // 4] = jnp.where(core == 0, low, high)
            give_ref[far, z % 4, z // 4] = jnp.where(core == 0, high, low)


def weight_term(place, pieces, att):
    half = jax.ShapeDtypeStruct((2, 4, 4, ROWS, COLS), jnp.bfloat16)
    return pl.pallas_call(
        term_kernel,
        out_shape=(half, half),
        in_specs=[pl.BlockSpec(memory_space=pltpu.SMEM)]
        + [pl.BlockSpec(memory_space=pl.ANY)] * SP
        + [pl.BlockSpec(memory_space=pltpu.VMEM)],
        out_specs=(
            pl.BlockSpec(memory_space=pltpu.VMEM),
            pl.BlockSpec(memory_space=pltpu.VMEM),
        ),
        scratch_shapes=[
            pltpu.VMEM((SP * IMG, D), jnp.bfloat16),
            pltpu.SemaphoreType.DMA((SP,)),
        ],
        compiler_params=pltpu.CompilerParams(vmem_limit_bytes=VMEM_LIMIT),
        cost_estimate=LIGHT,
        name="weight_term",
    )(place, *pieces, att)


def head_backward(window, joint, grad, att, probs, slopes, out_ref, out_window):
    keys, values = joint[1, :, window], joint[2, :, window]
    keys_t = transposed(keys).astype(jnp.bfloat16)

    def put(member, first, block):
        for r in range(SP):
            lo, hi = r * TXT - first, (r + 1) * TXT - first
            if 0 <= lo < block.shape[0]:
                out_ref[r, member, :TXT, out_window] = block[lo:hi]
            lo, hi = ALL_TXT + r * IMG - first, ALL_TXT + (r + 1) * IMG - first
            start, stop = max(lo, 0), min(hi, block.shape[0])
            if start < stop:
                rows = slice(TXT + start - lo, TXT + stop - lo)
                out_ref[r, member, rows, out_window] = block[start:stop]

    for chunk in range(LENGTH // CHUNK):
        rows = slice(chunk * CHUNK, (chunk + 1) * CHUNK)
        out_grad = grad[rows]
        product = out_grad.astype(jnp.float32) * att[rows].astype(jnp.float32)
        delta = jnp.sum(product.T, axis=0, keepdims=True)
        change = dot_last(values, out_grad) - delta
        slope = (probs[:, rows].astype(jnp.float32) * change).astype(jnp.bfloat16)
        slopes[:, rows] = slope
        put(0, chunk * CHUNK, (dot(keys_t, slope) * FACTOR).T.astype(jnp.bfloat16))
    put(1, 0, (dot(slopes[...], joint[0, :, window]) * FACTOR).astype(jnp.bfloat16))
    put(2, 0, dot(probs[...], grad[...]).astype(jnp.bfloat16))


def first_kernel(place_ref, *refs):
    pieces, rest = refs[:SP], refs[SP:]
    w_ref, x_ref, probs_ref, att, out_ref, other_ref = rest[:6]
    grad, text, image, weight, joint, probs, slopes, sems, dy_sems, qkv_sems = rest[6:]
    copies = [
        pltpu.make_async_copy(
            w_ref.at[:, x_lo, stream], weight.at[stream, x_lo], sems.at[2 * stream + x_lo]
        )
        for stream in range(2)
        for x_lo in range(2)
    ]
    for copy in copies[2:]:
        copy.start()
    dy_copies = load_dy(place_ref, pieces, text, image, dy_sems)
    for copy in copies[:2]:
        copy.start()
    late = load_qkv(x_ref, joint, qkv_sems)
    late.append(pltpu.make_async_copy(probs_ref.at[0], probs, sems.at[4]))
    late[-1].start()
    for copy in copies[2:] + dy_copies[:SP]:
        copy.wait()
    both = dot(image[...], weight[1].reshape(D, COLS)).astype(jnp.bfloat16)
    grad[ALL_TXT:, :] = both[:, :HD]
    other_ref[ALL_TXT:, :] = both[:, HD:]
    for copy in copies[:2] + dy_copies[SP:]:
        copy.wait()
    both = dot(text[...], weight[0].reshape(D, COLS)).astype(jnp.bfloat16)
    grad[:ALL_TXT, :] = both[:, :HD]
    other_ref[:ALL_TXT, :] = both[:, HD:]
    for copy in late:
        copy.wait()
    head_backward(slice(0, HD), joint, grad, att[:, :HD], probs, slopes, out_ref, slice(0, HD))


def second_kernel(x_ref, probs_ref, first_ref, grad, att, out_ref, *rest):
    joint, probs, slopes, sems, qkv_sems = rest
    copies = load_qkv(x_ref, joint, qkv_sems)
    copies.append(pltpu.make_async_copy(probs_ref.at[1], probs, sems.at[0]))
    copies[-1].start()
    out_ref[:, :, :, :HD] = first_ref[...]
    for copy in copies:
        copy.wait()
    window = slice(HD, COLS)
    head_backward(window, joint, grad, att[:, HD:], probs, slopes, out_ref, window)


ANY = pl.BlockSpec(memory_space=pl.ANY)
VMEM = pl.BlockSpec(memory_space=pltpu.VMEM)


def backward_first(place, pieces, w, x, probs, att):
    return pl.pallas_call(
        first_kernel,
        out_shape=(
            jax.ShapeDtypeStruct((SP, 3, TOK, HD), jnp.bfloat16),
            jax.ShapeDtypeStruct((LENGTH, HD), jnp.bfloat16),
        ),
        in_specs=[pl.BlockSpec(memory_space=pltpu.SMEM)] + [ANY] * (SP + 3) + [VMEM],
        out_specs=(VMEM, VMEM),
        scratch_shapes=[
            pltpu.VMEM((LENGTH, HD), jnp.bfloat16),
            pltpu.VMEM((ALL_TXT, D), jnp.bfloat16),
            pltpu.VMEM((ALL_IMG, D), jnp.bfloat16),
            pltpu.VMEM((2, 2, 32, ROWS, COLS), jnp.bfloat16),
            pltpu.VMEM((3, LENGTH, COLS), jnp.bfloat16),
            pltpu.VMEM((LENGTH, LENGTH), jnp.bfloat16),
            pltpu.VMEM((LENGTH, LENGTH), jnp.bfloat16),
            pltpu.SemaphoreType.DMA((5,)),
            pltpu.SemaphoreType.DMA((2 * SP,)),
            pltpu.SemaphoreType.DMA((2 * SP,)),
        ],
        compiler_params=pltpu.CompilerParams(vmem_limit_bytes=VMEM_LIMIT),
        cost_estimate=LIGHT,
        name="project_and_backward_first_head",
    )(place, *pieces, w, x, probs, att)


def backward_second(x, probs, first, grad, att):
    return pl.pallas_call(
        second_kernel,
        out_shape=jax.ShapeDtypeStruct((SP, 3, TOK, COLS), jnp.bfloat16),
        in_specs=[ANY] * 2 + [VMEM] * 3,
        out_specs=VMEM,
        scratch_shapes=[
            pltpu.VMEM((3, LENGTH, COLS), jnp.bfloat16),
            pltpu.VMEM((LENGTH, LENGTH), jnp.bfloat16),
            pltpu.VMEM((LENGTH, LENGTH), jnp.bfloat16),
            pltpu.SemaphoreType.DMA((1,)),
            pltpu.SemaphoreType.DMA((2 * SP,)),
        ],
        compiler_params=pltpu.CompilerParams(vmem_limit_bytes=VMEM_LIMIT),
        cost_estimate=LIGHT,
        name="backward_second_head",
    )(x, probs, first, grad, att)


def spread_kernel(back_ref, txt_ref, img_ref):
    for r in range(SP):
        columns = slice(r * COLS, (r + 1) * COLS)
        txt_ref[0, :, :, columns] = back_ref[r, :, :TXT, :]
        img_ref[0, :, :, columns] = back_ref[r, :, TXT:, :]


def spread(back):
    return pl.pallas_call(
        spread_kernel,
        out_shape=(
            jax.ShapeDtypeStruct((1, 3, TXT, SP * COLS), jnp.bfloat16),
            jax.ShapeDtypeStruct((1, 3, IMG, SP * COLS), jnp.bfloat16),
        ),
        in_specs=[VMEM],
        out_specs=(VMEM, VMEM),
        compiler_params=pltpu.CompilerParams(vmem_limit_bytes=VMEM_LIMIT),
        cost_estimate=LIGHT,
        name="spread_features",
    )(back)


def gather_weights(wv_txt, sc_txt, wv_img, sc_img, x_lo):
    own = jnp.stack([dequant(wv_txt, sc_txt), dequant(wv_img, sc_img)])
    other = send(own, SWAP_X_LO)
    pair = jnp.where(x_lo == 0, jnp.stack([own, other]), jnp.stack([other, own]))
    return lax.all_gather(pair, AXES, axis=0, axis_index_groups=Z_CORE_GROUPS)


def local(qkv_txt, qkv_img, dy_txt, dy_img, wv_txt, sc_txt, wv_img, sc_img):
    fsdp, sp = lax.axis_index("fsdp"), lax.axis_index("sp")
    core, x_lo, z = fsdp % 2, fsdp // 32, (fsdp // 2) % 16
    place = jnp.stack(slots(sp) + [core, x_lo]).astype(jnp.int32)

    own = jnp.concatenate([dy_txt[0], dy_img[0]], axis=0)
    by_y = {k: send(own, FROM_Y[k]) for k in (1, 2, 3)}
    across = send(own, SWAP_X_HI)

    x = jnp.concatenate(
        [qkv_txt[0].reshape(3, TXT, SP, COLS), qkv_img[0].reshape(3, IMG, SP, COLS)], axis=1
    ).transpose(2, 0, 1, 3)
    x, wv_txt, wv_img = lax.optimization_barrier((x, wv_txt, wv_img))
    w = gather_weights(wv_txt, sc_txt, wv_img, sc_img, x_lo)
    x = lax.all_to_all(x, "sp", 0, 0, tiled=True)
    att, probs = forward(x)

    pieces = [own, by_y[1], by_y[2], by_y[3]] + [
        across,
        send(across, FROM_Y[1]),
        send(by_y[2], SWAP_X_HI),
        send(across, FROM_Y[3]),
    ]
    keep, give = weight_term(place, pieces, att)

    other = send(give, SWAP_CORE)
    other, att = lax.optimization_barrier((other, att))
    far = send(plus(keep[1], other[1]).astype(jnp.bfloat16), SWAP_X_LO)
    first, grad = backward_first(place, pieces, w, x, probs, att)
    first, far = lax.optimization_barrier((first, far))
    part = plus(plus(keep[0], other[0]), far).astype(jnp.bfloat16)
    quads = lax.all_to_all(part, AXES, 0, 0, axis_index_groups=Z_NEAR_GROUPS, tiled=True)
    quads = jnp.sum(quads.astype(jnp.float32), axis=0).astype(jnp.bfloat16)
    back = backward_second(x, probs, first, grad, att)
    back, quads = lax.optimization_barrier((back, quads))
    back = lax.all_to_all(back, "sp", 0, 0, tiled=True)

    def quad(step):
        return lax.dynamic_index_in_dim(quads, (z // 4 + step) % 4, 0, keepdims=False)

    weight_grad = quad(0).astype(jnp.float32)
    for step in (1, 3, 2):
        weight_grad = weight_grad + send(quad(step), TO_Z[4 * step]).astype(jnp.float32)
    return (*spread(back), weight_grad * (1.0 / 64))


def solution(mesh):
    placed = (
        P("fsdp", None, "sp", None),
        P("fsdp", None, "sp", None),
        P("fsdp", "sp", None),
        P("fsdp", "sp", None),
        P("fsdp", "sp"),
        P("fsdp", "sp"),
        P("fsdp", "sp"),
        P("fsdp", "sp"),
    )
    return jax.shard_map(
        local,
        mesh=mesh,
        in_specs=placed,
        out_specs=(P("fsdp", None, "sp", None), P("fsdp", None, "sp", None), P("fsdp", "sp")),
        check_vma=False,
    )
```

```python
import functools
import math

import jax
import jax.numpy as jnp
from jax import lax
from jax.experimental import pallas as pl
from jax.experimental.pallas import tpu as pltpu
from jax.sharding import PartitionSpec as P

HD = 128
SP = 8
TXT = 32
IMG = 96
TOK = TXT + IMG
ALL_TXT = SP * TXT
ALL_IMG = SP * IMG
LENGTH = SP * TOK
COLS = 256
D = 3072
HALF = D // 2
ROWS = 48
HEADS = COLS // HD
CHUNK = 256
FACTOR = 1.0 / math.sqrt(HD)
LOG2E = 1.4426950408889634
SCALE2 = FACTOR * LOG2E
AXES = ("fsdp", "sp")
VMEM_LIMIT = 48 * 1024 * 1024
LIGHT = pl.CostEstimate(flops=1000, bytes_accessed=1000, transcendentals=0)


def number(x_lo, z, core, y, x_hi):
    return ((x_lo * 16 + z) * 2 + core) * SP + y * 2 + x_hi


def every():
    return [
        (x_lo, z, core, y, x_hi)
        for x_lo in range(2)
        for z in range(16)
        for core in range(2)
        for y in range(4)
        for x_hi in range(2)
    ]


def route(target):
    return [(number(*d), number(*target(*d))) for d in every()]


SWAP_CORE = route(lambda x_lo, z, core, y, x_hi: (x_lo, z, 1 - core, y, x_hi))
SWAP_X_LO = route(lambda x_lo, z, core, y, x_hi: (1 - x_lo, z, core, y, x_hi))
SWAP_X_HI = route(lambda x_lo, z, core, y, x_hi: (x_lo, z, core, y, 1 - x_hi))
FROM_Y = {
    k: route(lambda x_lo, z, core, y, x_hi, k=k: (x_lo, z, core, (y - k) % 4, x_hi))
    for k in (1, 3)
}
TO_Z = {
    k: route(lambda x_lo, z, core, y, x_hi, d=d: (x_lo, (z + d) % 16, core, y, x_hi))
    for k, d in ((4, 4), (8, 8), (12, -4))
}
NEAR_GROUPS = [
    [number(x_lo, 4 * quad + z, core, y, x_hi) for x_lo in range(2) for z in range(4)]
    for quad in range(4)
    for core in range(2)
    for y in range(4)
    for x_hi in range(2)
]
Z_CORE_GROUPS = [
    [number(x_lo, z, core, y, x_hi) for z in range(16) for core in range(2)]
    for x_lo in range(2)
    for y in range(4)
    for x_hi in range(2)
]


def send(x, pairs):
    return lax.ppermute(x, AXES, pairs)


def dequant(values, scales):
    return (values.astype(jnp.float32) * jnp.repeat(scales, HD, axis=1)).astype(jnp.bfloat16)


def plus(a, b):
    return a.astype(jnp.float32) + b.astype(jnp.float32)


def dot(a, b):
    return jnp.dot(a, b, preferred_element_type=jnp.float32)


def dot_last(a, b):
    return lax.dot_general(a, b, (((1,), (1,)), ((), ())), preferred_element_type=jnp.float32)


def transposed(x):
    return x.astype(jnp.float32).T


def load_qkv(x_ref, joint, sems):
    copies = []
    for r in range(SP):
        copies.append(
            pltpu.make_async_copy(
                x_ref.at[r, :, pl.ds(0, TXT), :],
                joint.at[:, pl.ds(r * TXT, TXT), :],
                sems.at[2 * r],
            )
        )
        copies.append(
            pltpu.make_async_copy(
                x_ref.at[r, :, pl.ds(TXT, IMG), :],
                joint.at[:, pl.ds(ALL_TXT + r * IMG, IMG), :],
                sems.at[2 * r + 1],
            )
        )
    for copy in copies:
        copy.start()
    return copies


def forward_kernel(x_ref, att_ref, probs_ref, joint, sems):
    for copy in load_qkv(x_ref, joint, sems):
        copy.wait()
    for head in range(HEADS):
        window = slice(head * HD, (head + 1) * HD)
        keys = joint[1, :, window]
        values_t = transposed(joint[2, :, window]).astype(jnp.bfloat16)
        for chunk in range(LENGTH // CHUNK):
            rows = slice(chunk * CHUNK, (chunk + 1) * CHUNK)
            scores = dot_last(keys, joint[0, rows, window])
            highest = jnp.max(scores, axis=0, keepdims=True)
            weights = jnp.exp2((scores - highest) * SCALE2)
            share = 1.0 / jnp.sum(weights, axis=0, keepdims=True)
            probs = (weights * share).astype(jnp.bfloat16)
            probs_ref[head, :, rows] = probs
            att_ref[rows, window] = dot(values_t, probs).T.astype(jnp.bfloat16)


def forward(x):
    return pl.pallas_call(
        forward_kernel,
        out_shape=(
            jax.ShapeDtypeStruct((LENGTH, COLS), jnp.bfloat16),
            jax.ShapeDtypeStruct((HEADS, LENGTH, LENGTH), jnp.bfloat16),
        ),
        in_specs=[pl.BlockSpec(memory_space=pl.ANY)],
        out_specs=(
            pl.BlockSpec(memory_space=pltpu.VMEM),
            pl.BlockSpec(memory_space=pltpu.VMEM),
        ),
        scratch_shapes=[
            pltpu.VMEM((3, LENGTH, COLS), jnp.bfloat16),
            pltpu.SemaphoreType.DMA((2 * SP,)),
        ],
        compiler_params=pltpu.CompilerParams(vmem_limit_bytes=VMEM_LIMIT),
        cost_estimate=LIGHT,
        name="attention_forward",
    )(x)


def slots(sp):
    y, x_hi = sp // 2, sp % 2
    return [((y + k) % 4) * 2 + x_hi for k in range(4)] + [
        ((y + k) % 4) * 2 + 1 - x_hi for k in range(4)
    ]


def load_dy(place_ref, pieces, text, image, sems):
    copies = []
    for target, row, size in [(image, TXT, IMG)] + ([(text, 0, TXT)] if text is not None else []):
        for n, piece in enumerate(pieces):
            rows = pl.ds(pl.multiple_of(place_ref[n] * size, TXT), size)
            if n % 4 == 2:
                ends = [
                    (piece.at[half, pl.ds(row, size), :], target.at[rows, pl.ds(half * HALF, HALF)])
                    for half in range(2)
                ]
            else:
                ends = [(piece.at[pl.ds(row, size), :], target.at[rows, :])]
            for source, place in ends:
                copies.append(pltpu.make_async_copy(source, place, sems.at[len(copies)]))
    for copy in copies:
        copy.start()
    return copies


BAND = 8 * 2 * ROWS


def term_kernel(place_ref, *refs):
    pieces, (att_ref, keep_ref, give_ref, image, sems) = refs[:SP], refs[SP:]
    copies = load_dy(place_ref, pieces, None, image, sems)
    att_t = transposed(att_ref[ALL_TXT:, :]).astype(jnp.bfloat16)
    for copy in copies:
        copy.wait()
    core = place_ref[SP]
    for band in range(D // BAND):
        term = dot(att_t, image[:, band * BAND : (band + 1) * BAND]).T.astype(jnp.bfloat16)
        for j in range(8):
            z = (band % 2) * 8 + j
            low = term[(2 * j) * ROWS : (2 * j + 1) * ROWS]
            high = term[(2 * j + 1) * ROWS : (2 * j + 2) * ROWS]
            keep_ref[4 * (band // 2) + z % 4, z // 4] = jnp.where(core == 0, low, high)
            give_ref[4 * (band // 2) + z % 4, z // 4] = jnp.where(core == 0, high, low)


def weight_term(place, pieces, att):
    half = jax.ShapeDtypeStruct((8, 4, ROWS, COLS), jnp.bfloat16)
    return pl.pallas_call(
        term_kernel,
        out_shape=(half, half),
        in_specs=[pl.BlockSpec(memory_space=pltpu.SMEM)]
        + [pl.BlockSpec(memory_space=pl.ANY)] * SP
        + [pl.BlockSpec(memory_space=pltpu.VMEM)],
        out_specs=(
            pl.BlockSpec(memory_space=pltpu.VMEM),
            pl.BlockSpec(memory_space=pltpu.VMEM),
        ),
        scratch_shapes=[
            pltpu.VMEM((SP * IMG, D), jnp.bfloat16),
            pltpu.SemaphoreType.DMA((SP + 2,)),
        ],
        compiler_params=pltpu.CompilerParams(vmem_limit_bytes=VMEM_LIMIT),
        cost_estimate=LIGHT,
        name="weight_term",
    )(place, *pieces, att)


def head_backward(window, joint, grad, att, probs, slopes, out_ref, out_window):
    keys, values = joint[1, :, window], joint[2, :, window]
    keys_t = transposed(keys).astype(jnp.bfloat16)

    def put(member, first, block):
        for r in range(SP):
            lo, hi = r * TXT - first, (r + 1) * TXT - first
            if 0 <= lo < block.shape[0]:
                out_ref[r, member, :TXT, out_window] = block[lo:hi]
            lo, hi = ALL_TXT + r * IMG - first, ALL_TXT + (r + 1) * IMG - first
            start, stop = max(lo, 0), min(hi, block.shape[0])
            if start < stop:
                rows = slice(TXT + start - lo, TXT + stop - lo)
                out_ref[r, member, rows, out_window] = block[start:stop]

    for chunk in range(LENGTH // CHUNK):
        rows = slice(chunk * CHUNK, (chunk + 1) * CHUNK)
        out_grad = grad[rows]
        product = out_grad.astype(jnp.float32) * att[rows].astype(jnp.float32)
        delta = jnp.sum(product.T, axis=0, keepdims=True)
        change = dot_last(values, out_grad) - delta
        slope = (probs[:, rows].astype(jnp.float32) * change).astype(jnp.bfloat16)
        slopes[:, rows] = slope
        put(0, chunk * CHUNK, (dot(keys_t, slope) * FACTOR).T.astype(jnp.bfloat16))
    put(1, 0, (dot(slopes[...], joint[0, :, window]) * FACTOR).astype(jnp.bfloat16))
    put(2, 0, dot(probs[...], grad[...]).astype(jnp.bfloat16))


def backward_kernel(place_ref, *refs):
    pieces, rest = refs[:SP], refs[SP:]
    w_ref, x_ref, probs_ref, att, out_ref = rest[:5]
    grad, text, image, weight, joint, probs, slopes, sems, dy_sems, qkv_sems = rest[5:]
    copies = [
        pltpu.make_async_copy(
            w_ref.at[:, x_lo, stream], weight.at[stream, x_lo], sems.at[2 * stream + x_lo]
        )
        for stream in range(2)
        for x_lo in range(2)
    ]
    for copy in copies[2:]:
        copy.start()
    dy_copies = load_dy(place_ref, pieces, text, image, dy_sems)
    for copy in copies[:2]:
        copy.start()
    late = load_qkv(x_ref, joint, qkv_sems)
    probs_copies = [
        pltpu.make_async_copy(probs_ref.at[head], probs.at[head], sems.at[4 + head])
        for head in range(HEADS)
    ]
    for copy in probs_copies:
        copy.start()
    for copy in copies[2:] + dy_copies[: SP + 2]:
        copy.wait()
    grad[ALL_TXT:, :] = dot(image[...], weight[1].reshape(D, COLS)).astype(jnp.bfloat16)
    for copy in copies[:2] + dy_copies[SP + 2 :]:
        copy.wait()
    grad[:ALL_TXT, :] = dot(text[...], weight[0].reshape(D, COLS)).astype(jnp.bfloat16)
    for copy in late:
        copy.wait()
    for head in range(HEADS):
        window = slice(head * HD, (head + 1) * HD)
        probs_copies[head].wait()
        head_backward(
            window, joint, grad[:, window], att[:, window], probs[head], slopes, out_ref, window
        )


ANY = pl.BlockSpec(memory_space=pl.ANY)
VMEM = pl.BlockSpec(memory_space=pltpu.VMEM)


def backward(place, pieces, w, x, probs, att):
    return pl.pallas_call(
        backward_kernel,
        out_shape=jax.ShapeDtypeStruct((SP, 3, TOK, COLS), jnp.bfloat16),
        in_specs=[pl.BlockSpec(memory_space=pltpu.SMEM)] + [ANY] * (SP + 3) + [VMEM],
        out_specs=VMEM,
        scratch_shapes=[
            pltpu.VMEM((LENGTH, COLS), jnp.bfloat16),
            pltpu.VMEM((ALL_TXT, D), jnp.bfloat16),
            pltpu.VMEM((ALL_IMG, D), jnp.bfloat16),
            pltpu.VMEM((2, 2, 32, ROWS, COLS), jnp.bfloat16),
            pltpu.VMEM((3, LENGTH, COLS), jnp.bfloat16),
            pltpu.VMEM((HEADS, LENGTH, LENGTH), jnp.bfloat16),
            pltpu.VMEM((LENGTH, LENGTH), jnp.bfloat16),
            pltpu.SemaphoreType.DMA((6,)),
            pltpu.SemaphoreType.DMA((2 * SP + 4,)),
            pltpu.SemaphoreType.DMA((2 * SP,)),
        ],
        compiler_params=pltpu.CompilerParams(vmem_limit_bytes=VMEM_LIMIT),
        cost_estimate=pl.CostEstimate(
            flops=HEADS * 8 * LENGTH * LENGTH * HD + 2 * LENGTH * D * COLS,
            bytes_accessed=LENGTH * D * 2 + 2 * D * COLS * 2 + 24 * LENGTH * LENGTH,
            transcendentals=0,
        ),
        name="project_and_backward",
    )(place, *pieces, w, x, probs, att)


def spread_kernel(back_ref, txt_ref, img_ref):
    for r in range(SP):
        columns = slice(r * COLS, (r + 1) * COLS)
        txt_ref[0, :, :, columns] = back_ref[r, :, :TXT, :]
        img_ref[0, :, :, columns] = back_ref[r, :, TXT:, :]


def spread(back):
    return pl.pallas_call(
        spread_kernel,
        out_shape=(
            jax.ShapeDtypeStruct((1, 3, TXT, SP * COLS), jnp.bfloat16),
            jax.ShapeDtypeStruct((1, 3, IMG, SP * COLS), jnp.bfloat16),
        ),
        in_specs=[VMEM],
        out_specs=(VMEM, VMEM),
        compiler_params=pltpu.CompilerParams(vmem_limit_bytes=VMEM_LIMIT),
        cost_estimate=LIGHT,
        name="spread_features",
    )(back)


def gather_weights(wv_txt, sc_txt, wv_img, sc_img, x_lo):
    own = jnp.stack([dequant(wv_txt, sc_txt), dequant(wv_img, sc_img)])
    other = send(own, SWAP_X_LO)
    pair = jnp.where(x_lo == 0, jnp.stack([own, other]), jnp.stack([other, own]))
    return lax.all_gather(pair, AXES, axis=0, axis_index_groups=Z_CORE_GROUPS)


def local(qkv_txt, qkv_img, dy_txt, dy_img, wv_txt, sc_txt, wv_img, sc_img):
    fsdp, sp = lax.axis_index("fsdp"), lax.axis_index("sp")
    core, x_lo, z = fsdp % 2, fsdp // 32, (fsdp // 2) % 16
    place = jnp.stack(slots(sp) + [core]).astype(jnp.int32)

    own = jnp.concatenate([dy_txt[0], dy_img[0]], axis=0)
    by_y = {k: send(own, FROM_Y[k]) for k in (1, 3)}
    across = send(own, SWAP_X_HI)

    x = jnp.concatenate(
        [qkv_txt[0].reshape(3, TXT, SP, COLS), qkv_img[0].reshape(3, IMG, SP, COLS)], axis=1
    ).transpose(2, 0, 1, 3)
    x, wv_txt, wv_img = lax.optimization_barrier((x, wv_txt, wv_img))
    w = gather_weights(wv_txt, sc_txt, wv_img, sc_img, x_lo)
    x = lax.all_to_all(x, "sp", 0, 0, tiled=True)
    att, probs = forward(x)

    far = jnp.stack(
        [send(by_y[1][:, :HALF], FROM_Y[1]), send(by_y[3][:, HALF:], FROM_Y[3])]
    )
    pieces = [own, by_y[1], far, by_y[3]] + [
        across,
        send(across, FROM_Y[1]),
        send(far, SWAP_X_HI),
        send(across, FROM_Y[3]),
    ]
    keep, give = weight_term(place, pieces, att)

    total = plus(keep, send(give, SWAP_CORE)).astype(jnp.bfloat16)
    total, att = lax.optimization_barrier((total, att))
    quads = lax.all_to_all(total, AXES, 0, 0, axis_index_groups=NEAR_GROUPS, tiled=True)
    back = backward(place, pieces, w, x, probs, att)
    back, quads = lax.optimization_barrier((back, quads))
    quads = jnp.sum(quads.astype(jnp.float32), axis=0).astype(jnp.bfloat16)
    back = lax.all_to_all(back, "sp", 0, 0, tiled=True)

    def quad(step):
        return lax.dynamic_index_in_dim(quads, (z // 4 + step) % 4, 0, keepdims=False)

    weight_grad = quad(0).astype(jnp.float32)
    for step in (1, 3, 2):
        weight_grad = weight_grad + send(quad(step), TO_Z[4 * step]).astype(jnp.float32)
    return (*spread(back), weight_grad * (1.0 / 64))


def solution(mesh):
    placed = (
        P("fsdp", None, "sp", None),
        P("fsdp", None, "sp", None),
        P("fsdp", "sp", None),
        P("fsdp", "sp", None),
        P("fsdp", "sp"),
        P("fsdp", "sp"),
        P("fsdp", "sp"),
        P("fsdp", "sp"),
    )
    return jax.shard_map(
        local,
        mesh=mesh,
        in_specs=placed,
        out_specs=(P("fsdp", None, "sp", None), P("fsdp", None, "sp", None), P("fsdp", "sp")),
        check_vma=False,
    )
```

```python
import functools
import math

import jax
import jax.numpy as jnp
from jax import lax
from jax.experimental import pallas as pl
from jax.experimental.pallas import tpu as pltpu
from jax.sharding import PartitionSpec as P

HD = 128
SP = 8
TXT = 32
IMG = 96
TOK = TXT + IMG
ALL_TXT = SP * TXT
ALL_IMG = SP * IMG
LENGTH = SP * TOK
COLS = 256
D = 3072
HALF = D // 2
ROWS = 48
HEADS = COLS // HD
CHUNK = 256
FACTOR = 1.0 / math.sqrt(HD)
LOG2E = 1.4426950408889634
SCALE2 = FACTOR * LOG2E
AXES = ("fsdp", "sp")
VMEM_LIMIT = 48 * 1024 * 1024
LIGHT = pl.CostEstimate(flops=1000, bytes_accessed=1000, transcendentals=0)


def number(x_lo, z, core, y, x_hi):
    return ((x_lo * 16 + z) * 2 + core) * SP + y * 2 + x_hi


def every():
    return [
        (x_lo, z, core, y, x_hi)
        for x_lo in range(2)
        for z in range(16)
        for core in range(2)
        for y in range(4)
        for x_hi in range(2)
    ]


def route(target):
    return [(number(*d), number(*target(*d))) for d in every()]


SWAP_CORE = route(lambda x_lo, z, core, y, x_hi: (x_lo, z, 1 - core, y, x_hi))
SWAP_X_LO = route(lambda x_lo, z, core, y, x_hi: (1 - x_lo, z, core, y, x_hi))
SWAP_X_HI = route(lambda x_lo, z, core, y, x_hi: (x_lo, z, core, y, 1 - x_hi))
FROM_Y = {
    k: route(lambda x_lo, z, core, y, x_hi, k=k: (x_lo, z, core, (y - k) % 4, x_hi))
    for k in (1, 3)
}
SWAP_Z = {
    k: route(lambda x_lo, z, core, y, x_hi, k=k: (x_lo, z ^ k, core, y, x_hi)) for k in (4, 8)
}
NEAR_GROUPS = [
    [number(x_lo, 4 * quad + z, core, y, x_hi) for x_lo in range(2) for z in range(4)]
    for quad in range(4)
    for core in range(2)
    for y in range(4)
    for x_hi in range(2)
]
Z_CORE_GROUPS = [
    [number(x_lo, z, core, y, x_hi) for z in range(16) for core in range(2)]
    for x_lo in range(2)
    for y in range(4)
    for x_hi in range(2)
]


def send(x, pairs):
    return lax.ppermute(x, AXES, pairs)


def dequant(values, scales):
    return (values.astype(jnp.float32) * jnp.repeat(scales, HD, axis=1)).astype(jnp.bfloat16)


def plus(a, b):
    return a.astype(jnp.float32) + b.astype(jnp.float32)


def dot(a, b):
    return jnp.dot(a, b, preferred_element_type=jnp.float32)


def dot_last(a, b):
    return lax.dot_general(a, b, (((1,), (1,)), ((), ())), preferred_element_type=jnp.float32)


def transposed(x):
    return x.astype(jnp.float32).T


def load_qkv(x_ref, joint, sems):
    copies = []
    for r in range(SP):
        copies.append(
            pltpu.make_async_copy(
                x_ref.at[r, :, pl.ds(0, TXT), :],
                joint.at[:, pl.ds(r * TXT, TXT), :],
                sems.at[2 * r],
            )
        )
        copies.append(
            pltpu.make_async_copy(
                x_ref.at[r, :, pl.ds(TXT, IMG), :],
                joint.at[:, pl.ds(ALL_TXT + r * IMG, IMG), :],
                sems.at[2 * r + 1],
            )
        )
    for copy in copies:
        copy.start()
    return copies


def forward_kernel(x_ref, att_ref, probs_ref, joint, sems):
    for copy in load_qkv(x_ref, joint, sems):
        copy.wait()
    for head in range(HEADS):
        window = slice(head * HD, (head + 1) * HD)
        keys = joint[1, :, window]
        values_t = transposed(joint[2, :, window]).astype(jnp.bfloat16)
        for chunk in range(LENGTH // CHUNK):
            rows = slice(chunk * CHUNK, (chunk + 1) * CHUNK)
            scores = dot_last(keys, joint[0, rows, window])
            highest = jnp.max(scores, axis=0, keepdims=True)
            weights = jnp.exp2((scores - highest) * SCALE2)
            share = 1.0 / jnp.sum(weights, axis=0, keepdims=True)
            probs = (weights * share).astype(jnp.bfloat16)
            probs_ref[head, :, rows] = probs
            att_ref[rows, window] = dot(values_t, probs).T.astype(jnp.bfloat16)


def forward(x):
    return pl.pallas_call(
        forward_kernel,
        out_shape=(
            jax.ShapeDtypeStruct((LENGTH, COLS), jnp.bfloat16),
            jax.ShapeDtypeStruct((HEADS, LENGTH, LENGTH), jnp.bfloat16),
        ),
        in_specs=[pl.BlockSpec(memory_space=pl.ANY)],
        out_specs=(
            pl.BlockSpec(memory_space=pltpu.VMEM),
            pl.BlockSpec(memory_space=pltpu.VMEM),
        ),
        scratch_shapes=[
            pltpu.VMEM((3, LENGTH, COLS), jnp.bfloat16),
            pltpu.SemaphoreType.DMA((2 * SP,)),
        ],
        compiler_params=pltpu.CompilerParams(vmem_limit_bytes=VMEM_LIMIT),
        cost_estimate=LIGHT,
        name="attention_forward",
    )(x)


def slots(sp):
    y, x_hi = sp // 2, sp % 2
    return [((y + k) % 4) * 2 + x_hi for k in range(4)] + [
        ((y + k) % 4) * 2 + 1 - x_hi for k in range(4)
    ]


def load_dy(place_ref, pieces, text, image, sems):
    copies = []
    for target, row, size in [(image, TXT, IMG)] + ([(text, 0, TXT)] if text is not None else []):
        for n, piece in enumerate(pieces):
            rows = pl.ds(pl.multiple_of(place_ref[n] * size, TXT), size)
            if n % 4 == 2:
                ends = [
                    (piece.at[half, pl.ds(row, size), :], target.at[rows, pl.ds(half * HALF, HALF)])
                    for half in range(2)
                ]
            else:
                ends = [(piece.at[pl.ds(row, size), :], target.at[rows, :])]
            for source, place in ends:
                copies.append(pltpu.make_async_copy(source, place, sems.at[len(copies)]))
    for copy in copies:
        copy.start()
    return copies


BAND = 8 * 2 * ROWS


def term_kernel(place_ref, *refs):
    pieces, (att_ref, keep_ref, give_ref, image, sems) = refs[:SP], refs[SP:]
    copies = load_dy(place_ref, pieces, None, image, sems)
    att_t = transposed(att_ref[ALL_TXT:, :]).astype(jnp.bfloat16)
    for copy in copies:
        copy.wait()
    core = place_ref[SP]
    for band in range(D // BAND):
        term = dot(att_t, image[:, band * BAND : (band + 1) * BAND]).T.astype(jnp.bfloat16)
        for j in range(8):
            z = (band % 2) * 8 + j
            low = term[(2 * j) * ROWS : (2 * j + 1) * ROWS]
            high = term[(2 * j + 1) * ROWS : (2 * j + 2) * ROWS]
            keep_ref[4 * (band // 2) + z % 4, z // 4] = jnp.where(core == 0, low, high)
            give_ref[4 * (band // 2) + z % 4, z // 4] = jnp.where(core == 0, high, low)


def weight_term(place, pieces, att):
    half = jax.ShapeDtypeStruct((8, 4, ROWS, COLS), jnp.bfloat16)
    return pl.pallas_call(
        term_kernel,
        out_shape=(half, half),
        in_specs=[pl.BlockSpec(memory_space=pltpu.SMEM)]
        + [pl.BlockSpec(memory_space=pl.ANY)] * SP
        + [pl.BlockSpec(memory_space=pltpu.VMEM)],
        out_specs=(
            pl.BlockSpec(memory_space=pltpu.VMEM),
            pl.BlockSpec(memory_space=pltpu.VMEM),
        ),
        scratch_shapes=[
            pltpu.VMEM((SP * IMG, D), jnp.bfloat16),
            pltpu.SemaphoreType.DMA((SP + 2,)),
        ],
        compiler_params=pltpu.CompilerParams(vmem_limit_bytes=VMEM_LIMIT),
        cost_estimate=LIGHT,
        name="weight_term",
    )(place, *pieces, att)


def head_backward(window, joint, grad, att, probs, slopes, out_ref, out_window):
    keys, values = joint[1, :, window], joint[2, :, window]
    keys_t = transposed(keys).astype(jnp.bfloat16)

    def put(member, first, block):
        for r in range(SP):
            lo, hi = r * TXT - first, (r + 1) * TXT - first
            if 0 <= lo < block.shape[0]:
                out_ref[r, member, :TXT, out_window] = block[lo:hi]
            lo, hi = ALL_TXT + r * IMG - first, ALL_TXT + (r + 1) * IMG - first
            start, stop = max(lo, 0), min(hi, block.shape[0])
            if start < stop:
                rows = slice(TXT + start - lo, TXT + stop - lo)
                out_ref[r, member, rows, out_window] = block[start:stop]

    for chunk in range(LENGTH // CHUNK):
        rows = slice(chunk * CHUNK, (chunk + 1) * CHUNK)
        out_grad = grad[rows]
        product = out_grad.astype(jnp.float32) * att[rows].astype(jnp.float32)
        delta = jnp.sum(product.T, axis=0, keepdims=True)
        change = dot_last(values, out_grad) - delta
        slope = (probs[:, rows].astype(jnp.float32) * change).astype(jnp.bfloat16)
        slopes[:, rows] = slope
        put(0, chunk * CHUNK, (dot(keys_t, slope) * FACTOR).T.astype(jnp.bfloat16))
    put(1, 0, (dot(slopes[...], joint[0, :, window]) * FACTOR).astype(jnp.bfloat16))
    put(2, 0, dot(probs[...], grad[...]).astype(jnp.bfloat16))


def backward_kernel(place_ref, *refs):
    pieces, rest = refs[:SP], refs[SP:]
    w_ref, x_ref, probs_ref, att, out_ref = rest[:5]
    grad, text, image, weight, joint, probs, slopes, sems, dy_sems, qkv_sems = rest[5:]
    copies = [
        pltpu.make_async_copy(
            w_ref.at[:, x_lo, stream], weight.at[stream, x_lo], sems.at[2 * stream + x_lo]
        )
        for stream in range(2)
        for x_lo in range(2)
    ]
    for copy in copies[2:]:
        copy.start()
    dy_copies = load_dy(place_ref, pieces, text, image, dy_sems)
    for copy in copies[:2]:
        copy.start()
    late = load_qkv(x_ref, joint, qkv_sems)
    probs_copies = [
        pltpu.make_async_copy(probs_ref.at[head], probs.at[head], sems.at[4 + head])
        for head in range(HEADS)
    ]
    for copy in probs_copies:
        copy.start()
    for copy in copies[2:] + dy_copies[: SP + 2]:
        copy.wait()
    grad[ALL_TXT:, :] = dot(image[...], weight[1].reshape(D, COLS)).astype(jnp.bfloat16)
    for copy in copies[:2] + dy_copies[SP + 2 :]:
        copy.wait()
    grad[:ALL_TXT, :] = dot(text[...], weight[0].reshape(D, COLS)).astype(jnp.bfloat16)
    for copy in late:
        copy.wait()
    for head in range(HEADS):
        window = slice(head * HD, (head + 1) * HD)
        probs_copies[head].wait()
        head_backward(
            window, joint, grad[:, window], att[:, window], probs[head], slopes, out_ref, window
        )


ANY = pl.BlockSpec(memory_space=pl.ANY)
VMEM = pl.BlockSpec(memory_space=pltpu.VMEM)


def backward(place, pieces, w, x, probs, att):
    return pl.pallas_call(
        backward_kernel,
        out_shape=jax.ShapeDtypeStruct((SP, 3, TOK, COLS), jnp.bfloat16),
        in_specs=[pl.BlockSpec(memory_space=pltpu.SMEM)] + [ANY] * (SP + 3) + [VMEM],
        out_specs=VMEM,
        scratch_shapes=[
            pltpu.VMEM((LENGTH, COLS), jnp.bfloat16),
            pltpu.VMEM((ALL_TXT, D), jnp.bfloat16),
            pltpu.VMEM((ALL_IMG, D), jnp.bfloat16),
            pltpu.VMEM((2, 2, 32, ROWS, COLS), jnp.bfloat16),
            pltpu.VMEM((3, LENGTH, COLS), jnp.bfloat16),
            pltpu.VMEM((HEADS, LENGTH, LENGTH), jnp.bfloat16),
            pltpu.VMEM((LENGTH, LENGTH), jnp.bfloat16),
            pltpu.SemaphoreType.DMA((6,)),
            pltpu.SemaphoreType.DMA((2 * SP + 4,)),
            pltpu.SemaphoreType.DMA((2 * SP,)),
        ],
        compiler_params=pltpu.CompilerParams(vmem_limit_bytes=VMEM_LIMIT),
        cost_estimate=pl.CostEstimate(
            flops=HEADS * 8 * LENGTH * LENGTH * HD + 2 * LENGTH * D * COLS,
            bytes_accessed=LENGTH * D * 2 + 2 * D * COLS * 2 + 24 * LENGTH * LENGTH,
            transcendentals=0,
        ),
        name="project_and_backward",
    )(place, *pieces, w, x, probs, att)


def spread_kernel(back_ref, txt_ref, img_ref):
    for r in range(SP):
        columns = slice(r * COLS, (r + 1) * COLS)
        txt_ref[0, :, :, columns] = back_ref[r, :, :TXT, :]
        img_ref[0, :, :, columns] = back_ref[r, :, TXT:, :]


def spread(back):
    return pl.pallas_call(
        spread_kernel,
        out_shape=(
            jax.ShapeDtypeStruct((1, 3, TXT, SP * COLS), jnp.bfloat16),
            jax.ShapeDtypeStruct((1, 3, IMG, SP * COLS), jnp.bfloat16),
        ),
        in_specs=[VMEM],
        out_specs=(VMEM, VMEM),
        compiler_params=pltpu.CompilerParams(vmem_limit_bytes=VMEM_LIMIT),
        cost_estimate=LIGHT,
        name="spread_features",
    )(back)


def gather_weights(wv_txt, sc_txt, wv_img, sc_img, x_lo):
    own = jnp.stack([dequant(wv_txt, sc_txt), dequant(wv_img, sc_img)])
    other = send(own, SWAP_X_LO)
    pair = jnp.where(x_lo == 0, jnp.stack([own, other]), jnp.stack([other, own]))
    return lax.all_gather(pair, AXES, axis=0, axis_index_groups=Z_CORE_GROUPS)


def local(qkv_txt, qkv_img, dy_txt, dy_img, wv_txt, sc_txt, wv_img, sc_img):
    fsdp, sp = lax.axis_index("fsdp"), lax.axis_index("sp")
    core, x_lo, z = fsdp % 2, fsdp // 32, (fsdp // 2) % 16
    place = jnp.stack(slots(sp) + [core]).astype(jnp.int32)

    own = jnp.concatenate([dy_txt[0], dy_img[0]], axis=0)
    by_y = {k: send(own, FROM_Y[k]) for k in (1, 3)}
    across = send(own, SWAP_X_HI)

    x = jnp.concatenate(
        [qkv_txt[0].reshape(3, TXT, SP, COLS), qkv_img[0].reshape(3, IMG, SP, COLS)], axis=1
    ).transpose(2, 0, 1, 3)
    w = gather_weights(wv_txt, sc_txt, wv_img, sc_img, x_lo)
    x = lax.all_to_all(x, "sp", 0, 0, tiled=True)
    att, probs = forward(x)

    far = jnp.stack(
        [send(by_y[1][:, :HALF], FROM_Y[1]), send(by_y[3][:, HALF:], FROM_Y[3])]
    )
    pieces = [own, by_y[1], far, by_y[3]] + [
        across,
        send(across, FROM_Y[1]),
        send(far, SWAP_X_HI),
        send(across, FROM_Y[3]),
    ]
    keep, give = weight_term(place, pieces, att)

    total = plus(keep, send(give, SWAP_CORE)).astype(jnp.bfloat16)
    total, att = lax.optimization_barrier((total, att))
    quads = lax.all_to_all(total, AXES, 0, 0, axis_index_groups=NEAR_GROUPS, tiled=True)
    back = backward(place, pieces, w, x, probs, att)
    back, quads = lax.optimization_barrier((back, quads))
    quads = jnp.sum(quads.astype(jnp.float32), axis=0).astype(jnp.bfloat16)
    back = lax.all_to_all(back, "sp", 0, 0, tiled=True)

    half, row = z // 8, (z // 4) % 2
    quads = quads.reshape(2, 2, ROWS, COLS)
    give = lax.dynamic_index_in_dim(quads, 1 - half, 0, keepdims=False)
    keep = lax.dynamic_index_in_dim(quads, half, 0, keepdims=False)
    pair = plus(keep, send(give, SWAP_Z[8]))
    give = lax.dynamic_index_in_dim(pair, 1 - row, 0, keepdims=False).astype(jnp.bfloat16)
    last = send(give, SWAP_Z[4])
    outs, last = lax.optimization_barrier((spread(back), last))
    keep = lax.dynamic_index_in_dim(pair, row, 0, keepdims=False)
    return (*outs, plus(keep, last) * (1.0 / 64))


def solution(mesh):
    placed = (
        P("fsdp", None, "sp", None),
        P("fsdp", None, "sp", None),
        P("fsdp", "sp", None),
        P("fsdp", "sp", None),
        P("fsdp", "sp"),
        P("fsdp", "sp"),
        P("fsdp", "sp"),
        P("fsdp", "sp"),
    )
    return jax.shard_map(
        local,
        mesh=mesh,
        in_specs=placed,
        out_specs=(P("fsdp", None, "sp", None), P("fsdp", None, "sp", None), P("fsdp", "sp")),
        check_vma=False,
    )
```

```python
import functools
import math

import jax
import jax.numpy as jnp
from jax import lax
from jax.experimental import pallas as pl
from jax.experimental.pallas import tpu as pltpu
from jax.sharding import PartitionSpec as P

HD = 128
SP = 8
TXT = 32
IMG = 96
TOK = TXT + IMG
ALL_TXT = SP * TXT
ALL_IMG = SP * IMG
LENGTH = SP * TOK
COLS = 256
D = 3072
HALF = D // 2
ROWS = 48
HEADS = COLS // HD
CHUNK = 256
FACTOR = 1.0 / math.sqrt(HD)
LOG2E = 1.4426950408889634
SCALE2 = FACTOR * LOG2E
AXES = ("fsdp", "sp")
VMEM_LIMIT = 48 * 1024 * 1024
LIGHT = pl.CostEstimate(flops=1000, bytes_accessed=1000, transcendentals=0)


def number(x_lo, z, core, y, x_hi):
    return ((x_lo * 16 + z) * 2 + core) * SP + y * 2 + x_hi


def every():
    return [
        (x_lo, z, core, y, x_hi)
        for x_lo in range(2)
        for z in range(16)
        for core in range(2)
        for y in range(4)
        for x_hi in range(2)
    ]


def route(target):
    return [(number(*d), number(*target(*d))) for d in every()]


SWAP_CORE = route(lambda x_lo, z, core, y, x_hi: (x_lo, z, 1 - core, y, x_hi))
SWAP_X_LO = route(lambda x_lo, z, core, y, x_hi: (1 - x_lo, z, core, y, x_hi))
SWAP_X_HI = route(lambda x_lo, z, core, y, x_hi: (x_lo, z, core, y, 1 - x_hi))
FROM_Y = {
    k: route(lambda x_lo, z, core, y, x_hi, k=k: (x_lo, z, core, (y - k) % 4, x_hi))
    for k in (1, 3)
}
SWAP_Z = {
    k: route(lambda x_lo, z, core, y, x_hi, k=k: (x_lo, z ^ k, core, y, x_hi)) for k in (4, 8)
}
NEAR_GROUPS = [
    [number(x_lo, 4 * quad + z, core, y, x_hi) for x_lo in range(2) for z in range(4)]
    for quad in range(4)
    for core in range(2)
    for y in range(4)
    for x_hi in range(2)
]
Z_CORE_GROUPS = [
    [number(x_lo, z, core, y, x_hi) for z in range(16) for core in range(2)]
    for x_lo in range(2)
    for y in range(4)
    for x_hi in range(2)
]


def send(x, pairs):
    return lax.ppermute(x, AXES, pairs)


def dequant(values, scales):
    return (values.astype(jnp.float32) * jnp.repeat(scales, HD, axis=1)).astype(jnp.bfloat16)


def plus(a, b):
    return a.astype(jnp.float32) + b.astype(jnp.float32)


def dot(a, b):
    return jnp.dot(a, b, preferred_element_type=jnp.float32)


def dot_last(a, b):
    return lax.dot_general(a, b, (((1,), (1,)), ((), ())), preferred_element_type=jnp.float32)


def transposed(x):
    return x.astype(jnp.float32).T


def load_qkv(x_ref, joint, sems):
    copies = []
    for r in range(SP):
        copies.append(
            pltpu.make_async_copy(
                x_ref.at[r, :, pl.ds(0, TXT), :],
                joint.at[:, pl.ds(r * TXT, TXT), :],
                sems.at[2 * r],
            )
        )
        copies.append(
            pltpu.make_async_copy(
                x_ref.at[r, :, pl.ds(TXT, IMG), :],
                joint.at[:, pl.ds(ALL_TXT + r * IMG, IMG), :],
                sems.at[2 * r + 1],
            )
        )
    for copy in copies:
        copy.start()
    return copies


def forward_kernel(x_ref, att_ref, probs_ref, joint, held, sems, out_sems):
    for copy in load_qkv(x_ref, joint, sems):
        copy.wait()
    copies = []
    for head in range(HEADS):
        window = slice(head * HD, (head + 1) * HD)
        keys = joint[1, :, window]
        values_t = transposed(joint[2, :, window]).astype(jnp.bfloat16)
        for chunk in range(LENGTH // CHUNK):
            rows = slice(chunk * CHUNK, (chunk + 1) * CHUNK)
            scores = dot_last(keys, joint[0, rows, window])
            highest = jnp.max(scores, axis=0, keepdims=True)
            weights = jnp.exp2((scores - highest) * SCALE2)
            share = 1.0 / jnp.sum(weights, axis=0, keepdims=True)
            probs = (weights * share).astype(jnp.bfloat16)
            held[head, :, rows] = probs
            copies.append(
                pltpu.make_async_copy(
                    held.at[head, :, pl.ds(chunk * CHUNK, CHUNK)],
                    probs_ref.at[head, :, pl.ds(chunk * CHUNK, CHUNK)],
                    out_sems.at[len(copies)],
                )
            )
            copies[-1].start()
            att_ref[rows, window] = dot(values_t, probs).T.astype(jnp.bfloat16)
    for copy in copies:
        copy.wait()


def forward(x):
    return pl.pallas_call(
        forward_kernel,
        out_shape=(
            jax.ShapeDtypeStruct((LENGTH, COLS), jnp.bfloat16),
            jax.ShapeDtypeStruct((HEADS, LENGTH, LENGTH), jnp.bfloat16),
        ),
        in_specs=[pl.BlockSpec(memory_space=pl.ANY)],
        out_specs=(
            pl.BlockSpec(memory_space=pltpu.VMEM),
            pl.BlockSpec(memory_space=pl.ANY),
        ),
        scratch_shapes=[
            pltpu.VMEM((3, LENGTH, COLS), jnp.bfloat16),
            pltpu.VMEM((HEADS, LENGTH, LENGTH), jnp.bfloat16),
            pltpu.SemaphoreType.DMA((2 * SP,)),
            pltpu.SemaphoreType.DMA((HEADS * LENGTH // CHUNK,)),
        ],
        compiler_params=pltpu.CompilerParams(vmem_limit_bytes=VMEM_LIMIT),
        cost_estimate=LIGHT,
        name="attention_forward",
    )(x)


def slots(sp):
    y, x_hi = sp // 2, sp % 2
    return [((y + k) % 4) * 2 + x_hi for k in range(4)] + [
        ((y + k) % 4) * 2 + 1 - x_hi for k in range(4)
    ]


def load_dy(place_ref, pieces, text, image, sems):
    copies = []
    for target, row, size in [(image, TXT, IMG)] + ([(text, 0, TXT)] if text is not None else []):
        for n, piece in enumerate(pieces):
            rows = pl.ds(pl.multiple_of(place_ref[n] * size, TXT), size)
            if n % 4 == 2:
                ends = [
                    (piece.at[half, pl.ds(row, size), :], target.at[rows, pl.ds(half * HALF, HALF)])
                    for half in range(2)
                ]
            else:
                ends = [(piece.at[pl.ds(row, size), :], target.at[rows, :])]
            for source, place in ends:
                copies.append(pltpu.make_async_copy(source, place, sems.at[len(copies)]))
    for copy in copies:
        copy.start()
    return copies


BAND = 8 * 2 * ROWS


def term_kernel(place_ref, *refs):
    pieces, (att_ref, keep_ref, give_ref, image, sems) = refs[:SP], refs[SP:]
    copies = load_dy(place_ref, pieces, None, image, sems)
    att_t = transposed(att_ref[ALL_TXT:, :]).astype(jnp.bfloat16)
    for copy in copies:
        copy.wait()
    core = place_ref[SP]
    for band in range(D // BAND):
        term = dot(att_t, image[:, band * BAND : (band + 1) * BAND]).T.astype(jnp.bfloat16)
        for j in range(8):
            z = (band % 2) * 8 + j
            low = term[(2 * j) * ROWS : (2 * j + 1) * ROWS]
            high = term[(2 * j + 1) * ROWS : (2 * j + 2) * ROWS]
            keep_ref[4 * (band // 2) + z % 4, z // 4] = jnp.where(core == 0, low, high)
            give_ref[4 * (band // 2) + z % 4, z // 4] = jnp.where(core == 0, high, low)


def weight_term(place, pieces, att):
    half = jax.ShapeDtypeStruct((8, 4, ROWS, COLS), jnp.bfloat16)
    return pl.pallas_call(
        term_kernel,
        out_shape=(half, half),
        in_specs=[pl.BlockSpec(memory_space=pltpu.SMEM)]
        + [pl.BlockSpec(memory_space=pl.ANY)] * SP
        + [pl.BlockSpec(memory_space=pltpu.VMEM)],
        out_specs=(
            pl.BlockSpec(memory_space=pltpu.VMEM),
            pl.BlockSpec(memory_space=pltpu.VMEM),
        ),
        scratch_shapes=[
            pltpu.VMEM((SP * IMG, D), jnp.bfloat16),
            pltpu.SemaphoreType.DMA((SP + 2,)),
        ],
        compiler_params=pltpu.CompilerParams(vmem_limit_bytes=VMEM_LIMIT),
        cost_estimate=LIGHT,
        name="weight_term",
    )(place, *pieces, att)


def head_backward(window, joint, grad, att, probs, slopes, out_ref, out_window):
    keys, values = joint[1, :, window], joint[2, :, window]
    keys_t = transposed(keys).astype(jnp.bfloat16)

    def put(member, first, block):
        for r in range(SP):
            lo, hi = r * TXT - first, (r + 1) * TXT - first
            if 0 <= lo < block.shape[0]:
                out_ref[r, member, :TXT, out_window] = block[lo:hi]
            lo, hi = ALL_TXT + r * IMG - first, ALL_TXT + (r + 1) * IMG - first
            start, stop = max(lo, 0), min(hi, block.shape[0])
            if start < stop:
                rows = slice(TXT + start - lo, TXT + stop - lo)
                out_ref[r, member, rows, out_window] = block[start:stop]

    for chunk in range(LENGTH // CHUNK):
        rows = slice(chunk * CHUNK, (chunk + 1) * CHUNK)
        out_grad = grad[rows]
        product = out_grad.astype(jnp.float32) * att[rows].astype(jnp.float32)
        delta = jnp.sum(product.T, axis=0, keepdims=True)
        change = dot_last(values, out_grad) - delta
        slope = (probs[:, rows].astype(jnp.float32) * change).astype(jnp.bfloat16)
        slopes[:, rows] = slope
        put(0, chunk * CHUNK, (dot(keys_t, slope) * FACTOR).T.astype(jnp.bfloat16))
    put(1, 0, (dot(slopes[...], joint[0, :, window]) * FACTOR).astype(jnp.bfloat16))
    put(2, 0, dot(probs[...], grad[...]).astype(jnp.bfloat16))


def backward_kernel(place_ref, *refs):
    pieces, rest = refs[:SP], refs[SP:]
    w_ref, x_ref, probs_ref, att, out_ref = rest[:5]
    grad, text, image, weight, joint, probs, slopes, sems, dy_sems, qkv_sems = rest[5:]
    copies = [
        pltpu.make_async_copy(
            w_ref.at[:, x_lo, stream], weight.at[stream, x_lo], sems.at[2 * stream + x_lo]
        )
        for stream in range(2)
        for x_lo in range(2)
    ]
    for copy in copies[2:]:
        copy.start()
    dy_copies = load_dy(place_ref, pieces, text, image, dy_sems)
    for copy in copies[:2]:
        copy.start()
    late = load_qkv(x_ref, joint, qkv_sems)
    probs_copies = [
        pltpu.make_async_copy(probs_ref.at[head], probs.at[head], sems.at[4 + head])
        for head in range(HEADS)
    ]
    for copy in probs_copies:
        copy.start()
    for copy in copies[2:] + dy_copies[: SP + 2]:
        copy.wait()
    grad[ALL_TXT:, :] = dot(image[...], weight[1].reshape(D, COLS)).astype(jnp.bfloat16)
    for copy in copies[:2] + dy_copies[SP + 2 :]:
        copy.wait()
    grad[:ALL_TXT, :] = dot(text[...], weight[0].reshape(D, COLS)).astype(jnp.bfloat16)
    for copy in late:
        copy.wait()
    for head in range(HEADS):
        window = slice(head * HD, (head + 1) * HD)
        probs_copies[head].wait()
        head_backward(
            window, joint, grad[:, window], att[:, window], probs[head], slopes, out_ref, window
        )


ANY = pl.BlockSpec(memory_space=pl.ANY)
VMEM = pl.BlockSpec(memory_space=pltpu.VMEM)


def backward(place, pieces, w, x, probs, att):
    return pl.pallas_call(
        backward_kernel,
        out_shape=jax.ShapeDtypeStruct((SP, 3, TOK, COLS), jnp.bfloat16),
        in_specs=[pl.BlockSpec(memory_space=pltpu.SMEM)] + [ANY] * (SP + 3) + [VMEM],
        out_specs=VMEM,
        scratch_shapes=[
            pltpu.VMEM((LENGTH, COLS), jnp.bfloat16),
            pltpu.VMEM((ALL_TXT, D), jnp.bfloat16),
            pltpu.VMEM((ALL_IMG, D), jnp.bfloat16),
            pltpu.VMEM((2, 2, 32, ROWS, COLS), jnp.bfloat16),
            pltpu.VMEM((3, LENGTH, COLS), jnp.bfloat16),
            pltpu.VMEM((HEADS, LENGTH, LENGTH), jnp.bfloat16),
            pltpu.VMEM((LENGTH, LENGTH), jnp.bfloat16),
            pltpu.SemaphoreType.DMA((6,)),
            pltpu.SemaphoreType.DMA((2 * SP + 4,)),
            pltpu.SemaphoreType.DMA((2 * SP,)),
        ],
        compiler_params=pltpu.CompilerParams(vmem_limit_bytes=VMEM_LIMIT),
        cost_estimate=pl.CostEstimate(
            flops=HEADS * 8 * LENGTH * LENGTH * HD + 2 * LENGTH * D * COLS,
            bytes_accessed=LENGTH * D * 2 + 2 * D * COLS * 2 + 24 * LENGTH * LENGTH,
            transcendentals=0,
        ),
        name="project_and_backward",
    )(place, *pieces, w, x, probs, att)


def spread_kernel(back_ref, txt_ref, img_ref):
    for r in range(SP):
        columns = slice(r * COLS, (r + 1) * COLS)
        txt_ref[0, :, :, columns] = back_ref[r, :, :TXT, :]
        img_ref[0, :, :, columns] = back_ref[r, :, TXT:, :]


def spread(back):
    return pl.pallas_call(
        spread_kernel,
        out_shape=(
            jax.ShapeDtypeStruct((1, 3, TXT, SP * COLS), jnp.bfloat16),
            jax.ShapeDtypeStruct((1, 3, IMG, SP * COLS), jnp.bfloat16),
        ),
        in_specs=[VMEM],
        out_specs=(VMEM, VMEM),
        compiler_params=pltpu.CompilerParams(vmem_limit_bytes=VMEM_LIMIT),
        cost_estimate=LIGHT,
        name="spread_features",
    )(back)


def gather_weights(wv_txt, sc_txt, wv_img, sc_img, x_lo):
    own = jnp.stack([dequant(wv_txt, sc_txt), dequant(wv_img, sc_img)])
    other = send(own, SWAP_X_LO)
    pair = jnp.where(x_lo == 0, jnp.stack([own, other]), jnp.stack([other, own]))
    return lax.all_gather(pair, AXES, axis=0, axis_index_groups=Z_CORE_GROUPS)


def local(qkv_txt, qkv_img, dy_txt, dy_img, wv_txt, sc_txt, wv_img, sc_img):
    fsdp, sp = lax.axis_index("fsdp"), lax.axis_index("sp")
    core, x_lo, z = fsdp % 2, fsdp // 32, (fsdp // 2) % 16
    place = jnp.stack(slots(sp) + [core]).astype(jnp.int32)

    own = jnp.concatenate([dy_txt[0], dy_img[0]], axis=0)
    by_y = {k: send(own, FROM_Y[k]) for k in (1, 3)}
    across = send(own, SWAP_X_HI)

    x = jnp.concatenate(
        [qkv_txt[0].reshape(3, TXT, SP, COLS), qkv_img[0].reshape(3, IMG, SP, COLS)], axis=1
    ).transpose(2, 0, 1, 3)
    w = gather_weights(wv_txt, sc_txt, wv_img, sc_img, x_lo)
    x = lax.all_to_all(x, "sp", 0, 0, tiled=True)
    att, probs = forward(x)

    far = jnp.stack(
        [send(by_y[1][:, :HALF], FROM_Y[1]), send(by_y[3][:, HALF:], FROM_Y[3])]
    )
    pieces = [own, by_y[1], far, by_y[3]] + [
        across,
        send(across, FROM_Y[1]),
        send(far, SWAP_X_HI),
        send(across, FROM_Y[3]),
    ]
    keep, give = weight_term(place, pieces, att)

    total = plus(keep, send(give, SWAP_CORE)).astype(jnp.bfloat16)
    total, att = lax.optimization_barrier((total, att))
    quads = lax.all_to_all(total, AXES, 0, 0, axis_index_groups=NEAR_GROUPS, tiled=True)
    back = backward(place, pieces, w, x, probs, att)
    back, quads = lax.optimization_barrier((back, quads))
    quads = jnp.sum(quads.astype(jnp.float32), axis=0).astype(jnp.bfloat16)
    back = lax.all_to_all(back, "sp", 0, 0, tiled=True)

    half, row = z // 8, (z // 4) % 2
    quads = quads.reshape(2, 2, ROWS, COLS)
    give = lax.dynamic_index_in_dim(quads, 1 - half, 0, keepdims=False)
    keep = lax.dynamic_index_in_dim(quads, half, 0, keepdims=False)
    pair = plus(keep, send(give, SWAP_Z[8]))
    give = lax.dynamic_index_in_dim(pair, 1 - row, 0, keepdims=False).astype(jnp.bfloat16)
    last = send(give, SWAP_Z[4])
    outs, last = lax.optimization_barrier((spread(back), last))
    keep = lax.dynamic_index_in_dim(pair, row, 0, keepdims=False)
    return (*outs, plus(keep, last) * (1.0 / 64))


def solution(mesh):
    placed = (
        P("fsdp", None, "sp", None),
        P("fsdp", None, "sp", None),
        P("fsdp", "sp", None),
        P("fsdp", "sp", None),
        P("fsdp", "sp"),
        P("fsdp", "sp"),
        P("fsdp", "sp"),
        P("fsdp", "sp"),
    )
    return jax.shard_map(
        local,
        mesh=mesh,
        in_specs=placed,
        out_specs=(P("fsdp", None, "sp", None), P("fsdp", None, "sp", None), P("fsdp", "sp")),
        check_vma=False,
    )
```

```python
import functools
import math

import jax
import jax.numpy as jnp
from jax import lax
from jax.experimental import pallas as pl
from jax.experimental.pallas import tpu as pltpu
from jax.sharding import PartitionSpec as P

HD = 128
SP = 8
TXT = 32
IMG = 96
TOK = TXT + IMG
ALL_TXT = SP * TXT
ALL_IMG = SP * IMG
LENGTH = SP * TOK
COLS = 256
D = 3072
HALF = D // 2
ROWS = 48
HEADS = COLS // HD
CHUNK = 256
FACTOR = 1.0 / math.sqrt(HD)
LOG2E = 1.4426950408889634
SCALE2 = FACTOR * LOG2E
AXES = ("fsdp", "sp")
VMEM_LIMIT = 48 * 1024 * 1024
LIGHT = pl.CostEstimate(flops=1000, bytes_accessed=1000, transcendentals=0)


def number(x_lo, z, core, y, x_hi):
    return ((x_lo * 16 + z) * 2 + core) * SP + y * 2 + x_hi


def every():
    return [
        (x_lo, z, core, y, x_hi)
        for x_lo in range(2)
        for z in range(16)
        for core in range(2)
        for y in range(4)
        for x_hi in range(2)
    ]


def route(target):
    return [(number(*d), number(*target(*d))) for d in every()]


SWAP_CORE = route(lambda x_lo, z, core, y, x_hi: (x_lo, z, 1 - core, y, x_hi))
SWAP_X_LO = route(lambda x_lo, z, core, y, x_hi: (1 - x_lo, z, core, y, x_hi))
SWAP_X_HI = route(lambda x_lo, z, core, y, x_hi: (x_lo, z, core, y, 1 - x_hi))
FROM_Y = {
    k: route(lambda x_lo, z, core, y, x_hi, k=k: (x_lo, z, core, (y - k) % 4, x_hi))
    for k in (1, 3)
}
SWAP_Z = {
    k: route(lambda x_lo, z, core, y, x_hi, k=k: (x_lo, z ^ k, core, y, x_hi)) for k in (4, 8)
}
NEAR_GROUPS = [
    [number(x_lo, 4 * quad + z, core, y, x_hi) for x_lo in range(2) for z in range(4)]
    for quad in range(4)
    for core in range(2)
    for y in range(4)
    for x_hi in range(2)
]
Z_CORE_GROUPS = [
    [number(x_lo, z, core, y, x_hi) for z in range(16) for core in range(2)]
    for x_lo in range(2)
    for y in range(4)
    for x_hi in range(2)
]


def send(x, pairs):
    return lax.ppermute(x, AXES, pairs)


def plus(a, b):
    return a.astype(jnp.float32) + b.astype(jnp.float32)


def dot(a, b):
    return jnp.dot(a, b, preferred_element_type=jnp.float32)


def dot_last(a, b):
    return lax.dot_general(a, b, (((1,), (1,)), ((), ())), preferred_element_type=jnp.float32)


def transposed(x):
    return x.astype(jnp.float32).T


def load_qkv(x_ref, joint, sems):
    copies = []
    for r in range(SP):
        copies.append(
            pltpu.make_async_copy(
                x_ref.at[r, :, pl.ds(0, TXT), :],
                joint.at[:, pl.ds(r * TXT, TXT), :],
                sems.at[2 * r],
            )
        )
        copies.append(
            pltpu.make_async_copy(
                x_ref.at[r, :, pl.ds(TXT, IMG), :],
                joint.at[:, pl.ds(ALL_TXT + r * IMG, IMG), :],
                sems.at[2 * r + 1],
            )
        )
    for copy in copies:
        copy.start()
    return copies


def forward_kernel(x_ref, att_ref, probs_ref, joint, sems):
    for copy in load_qkv(x_ref, joint, sems):
        copy.wait()
    for head in range(HEADS):
        window = slice(head * HD, (head + 1) * HD)
        keys = joint[1, :, window]
        values_t = transposed(joint[2, :, window]).astype(jnp.bfloat16)
        for chunk in range(LENGTH // CHUNK):
            rows = slice(chunk * CHUNK, (chunk + 1) * CHUNK)
            scores = dot_last(keys, joint[0, rows, window])
            highest = jnp.max(scores, axis=0, keepdims=True)
            weights = jnp.exp2((scores - highest) * SCALE2)
            share = 1.0 / jnp.sum(weights, axis=0, keepdims=True)
            probs = (weights * share).astype(jnp.bfloat16)
            probs_ref[head, :, rows] = probs
            att_ref[rows, window] = dot(values_t, probs).T.astype(jnp.bfloat16)


def forward(x):
    return pl.pallas_call(
        forward_kernel,
        out_shape=(
            jax.ShapeDtypeStruct((LENGTH, COLS), jnp.bfloat16),
            jax.ShapeDtypeStruct((HEADS, LENGTH, LENGTH), jnp.bfloat16),
        ),
        in_specs=[pl.BlockSpec(memory_space=pl.ANY)],
        out_specs=(
            pl.BlockSpec(memory_space=pltpu.VMEM),
            pl.BlockSpec(memory_space=pltpu.VMEM),
        ),
        scratch_shapes=[
            pltpu.VMEM((3, LENGTH, COLS), jnp.bfloat16),
            pltpu.SemaphoreType.DMA((2 * SP,)),
        ],
        compiler_params=pltpu.CompilerParams(vmem_limit_bytes=VMEM_LIMIT),
        cost_estimate=LIGHT,
        name="attention_forward",
    )(x)


def slots(sp):
    y, x_hi = sp // 2, sp % 2
    return [((y + k) % 4) * 2 + x_hi for k in range(4)] + [
        ((y + k) % 4) * 2 + 1 - x_hi for k in range(4)
    ]


def load_dy(place_ref, pieces, text, image, sems):
    copies = []
    for target, row, size in [(image, TXT, IMG)] + ([(text, 0, TXT)] if text is not None else []):
        for n, piece in enumerate(pieces):
            rows = pl.ds(pl.multiple_of(place_ref[n] * size, TXT), size)
            if n % 4 == 2:
                ends = [
                    (piece.at[half, pl.ds(row, size), :], target.at[rows, pl.ds(half * HALF, HALF)])
                    for half in range(2)
                ]
            else:
                ends = [(piece.at[pl.ds(row, size), :], target.at[rows, :])]
            for source, place in ends:
                copies.append(pltpu.make_async_copy(source, place, sems.at[len(copies)]))
    for copy in copies:
        copy.start()
    return copies


BAND = 8 * 2 * ROWS


def term_kernel(place_ref, *refs):
    pieces, (att_ref, keep_ref, give_ref, image, sems) = refs[:SP], refs[SP:]
    copies = load_dy(place_ref, pieces, None, image, sems)
    att_t = transposed(att_ref[ALL_TXT:, :]).astype(jnp.bfloat16)
    for copy in copies:
        copy.wait()
    core = place_ref[SP]
    for band in range(D // BAND):
        term = dot(att_t, image[:, band * BAND : (band + 1) * BAND]).T.astype(jnp.bfloat16)
        for j in range(8):
            z = (band % 2) * 8 + j
            low = term[(2 * j) * ROWS : (2 * j + 1) * ROWS]
            high = term[(2 * j + 1) * ROWS : (2 * j + 2) * ROWS]
            keep_ref[4 * (band // 2) + z % 4, z // 4] = jnp.where(core == 0, low, high)
            give_ref[4 * (band // 2) + z % 4, z // 4] = jnp.where(core == 0, high, low)


def weight_term(place, pieces, att):
    half = jax.ShapeDtypeStruct((8, 4, ROWS, COLS), jnp.bfloat16)
    return pl.pallas_call(
        term_kernel,
        out_shape=(half, half),
        in_specs=[pl.BlockSpec(memory_space=pltpu.SMEM)]
        + [pl.BlockSpec(memory_space=pl.ANY)] * SP
        + [pl.BlockSpec(memory_space=pltpu.VMEM)],
        out_specs=(
            pl.BlockSpec(memory_space=pltpu.VMEM),
            pl.BlockSpec(memory_space=pltpu.VMEM),
        ),
        scratch_shapes=[
            pltpu.VMEM((SP * IMG, D), jnp.bfloat16),
            pltpu.SemaphoreType.DMA((SP + 2,)),
        ],
        compiler_params=pltpu.CompilerParams(vmem_limit_bytes=VMEM_LIMIT),
        cost_estimate=LIGHT,
        name="weight_term",
    )(place, *pieces, att)


def head_backward(window, joint, grad, att, probs, slopes, out_ref, out_window):
    keys, values = joint[1, :, window], joint[2, :, window]
    keys_t = transposed(keys).astype(jnp.bfloat16)

    def put(member, first, block):
        for r in range(SP):
            lo, hi = r * TXT - first, (r + 1) * TXT - first
            if 0 <= lo < block.shape[0]:
                out_ref[r, member, :TXT, out_window] = block[lo:hi]
            lo, hi = ALL_TXT + r * IMG - first, ALL_TXT + (r + 1) * IMG - first
            start, stop = max(lo, 0), min(hi, block.shape[0])
            if start < stop:
                rows = slice(TXT + start - lo, TXT + stop - lo)
                out_ref[r, member, rows, out_window] = block[start:stop]

    for chunk in range(LENGTH // CHUNK):
        rows = slice(chunk * CHUNK, (chunk + 1) * CHUNK)
        out_grad = grad[rows]
        product = out_grad.astype(jnp.float32) * att[rows].astype(jnp.float32)
        delta = jnp.sum(product.T, axis=0, keepdims=True)
        change = dot_last(values, out_grad) - delta
        slope = (probs[:, rows].astype(jnp.float32) * change).astype(jnp.bfloat16)
        slopes[:, rows] = slope
        put(0, chunk * CHUNK, (dot(keys_t, slope) * FACTOR).T.astype(jnp.bfloat16))
    put(1, 0, (dot(slopes[...], joint[0, :, window]) * FACTOR).astype(jnp.bfloat16))
    put(2, 0, dot(probs[...], grad[...]).astype(jnp.bfloat16))


def backward_kernel(place_ref, *refs):
    pieces, rest = refs[:SP], refs[SP:]
    w_ref, x_ref, probs_ref, att, out_ref = rest[:5]
    grad, text, image, weight, joint, probs, slopes, sems, dy_sems, qkv_sems = rest[5:]
    x_lo = place_ref[SP + 1]
    copies = [
        pltpu.make_async_copy(
            w_ref.at[:, n, stream],
            weight.at[stream, (x_lo + n) % 2],
            sems.at[2 * stream + n],
        )
        for stream in range(2)
        for n in range(2)
    ]
    for copy in copies[2:]:
        copy.start()
    dy_copies = load_dy(place_ref, pieces, text, image, dy_sems)
    for copy in copies[:2]:
        copy.start()
    late = load_qkv(x_ref, joint, qkv_sems)
    probs_copies = [
        pltpu.make_async_copy(probs_ref.at[head], probs.at[head], sems.at[4 + head])
        for head in range(HEADS)
    ]
    for copy in probs_copies:
        copy.start()
    for copy in copies[2:] + dy_copies[: SP + 2]:
        copy.wait()
    grad[ALL_TXT:, :] = dot(image[...], weight[1].reshape(D, COLS)).astype(jnp.bfloat16)
    for copy in copies[:2] + dy_copies[SP + 2 :]:
        copy.wait()
    grad[:ALL_TXT, :] = dot(text[...], weight[0].reshape(D, COLS)).astype(jnp.bfloat16)
    for copy in late:
        copy.wait()
    for head in range(HEADS):
        window = slice(head * HD, (head + 1) * HD)
        probs_copies[head].wait()
        head_backward(
            window, joint, grad[:, window], att[:, window], probs[head], slopes, out_ref, window
        )


ANY = pl.BlockSpec(memory_space=pl.ANY)
VMEM = pl.BlockSpec(memory_space=pltpu.VMEM)


def backward(place, pieces, w, x, probs, att):
    return pl.pallas_call(
        backward_kernel,
        out_shape=jax.ShapeDtypeStruct((SP, 3, TOK, COLS), jnp.bfloat16),
        in_specs=[pl.BlockSpec(memory_space=pltpu.SMEM)] + [ANY] * (SP + 3) + [VMEM],
        out_specs=VMEM,
        scratch_shapes=[
            pltpu.VMEM((LENGTH, COLS), jnp.bfloat16),
            pltpu.VMEM((ALL_TXT, D), jnp.bfloat16),
            pltpu.VMEM((ALL_IMG, D), jnp.bfloat16),
            pltpu.VMEM((2, 2, 32, ROWS, COLS), jnp.bfloat16),
            pltpu.VMEM((3, LENGTH, COLS), jnp.bfloat16),
            pltpu.VMEM((HEADS, LENGTH, LENGTH), jnp.bfloat16),
            pltpu.VMEM((LENGTH, LENGTH), jnp.bfloat16),
            pltpu.SemaphoreType.DMA((6,)),
            pltpu.SemaphoreType.DMA((2 * SP + 4,)),
            pltpu.SemaphoreType.DMA((2 * SP,)),
        ],
        compiler_params=pltpu.CompilerParams(vmem_limit_bytes=VMEM_LIMIT),
        cost_estimate=pl.CostEstimate(
            flops=HEADS * 8 * LENGTH * LENGTH * HD + 2 * LENGTH * D * COLS,
            bytes_accessed=LENGTH * D * 2 + 2 * D * COLS * 2 + 24 * LENGTH * LENGTH,
            transcendentals=0,
        ),
        name="project_and_backward",
    )(place, *pieces, w, x, probs, att)


def spread_kernel(back_ref, txt_ref, img_ref):
    for r in range(SP):
        columns = slice(r * COLS, (r + 1) * COLS)
        txt_ref[0, :, :, columns] = back_ref[r, :, :TXT, :]
        img_ref[0, :, :, columns] = back_ref[r, :, TXT:, :]


def spread(back):
    return pl.pallas_call(
        spread_kernel,
        out_shape=(
            jax.ShapeDtypeStruct((1, 3, TXT, SP * COLS), jnp.bfloat16),
            jax.ShapeDtypeStruct((1, 3, IMG, SP * COLS), jnp.bfloat16),
        ),
        in_specs=[VMEM],
        out_specs=(VMEM, VMEM),
        compiler_params=pltpu.CompilerParams(vmem_limit_bytes=VMEM_LIMIT),
        cost_estimate=LIGHT,
        name="spread_features",
    )(back)


def dequant_kernel(txt_ref, txt_scales, img_ref, img_scales, out_ref):
    for stream, (values, scales) in enumerate(((txt_ref, txt_scales), (img_ref, img_scales))):
        by_row = scales[...].T
        for head in range(HEADS):
            window = slice(head * HD, (head + 1) * HD)
            scaled = values[:, window].astype(jnp.float32) * by_row[:, head : head + 1]
            out_ref[stream, :, window] = scaled.astype(jnp.bfloat16)


def dequant(wv_txt, sc_txt, wv_img, sc_img):
    return pl.pallas_call(
        dequant_kernel,
        out_shape=jax.ShapeDtypeStruct((2, ROWS, COLS), jnp.bfloat16),
        in_specs=[VMEM] * 4,
        out_specs=VMEM,
        cost_estimate=LIGHT,
        name="dequantize",
    )(wv_txt, sc_txt.T, wv_img, sc_img.T)


def gather_weights(own, other):
    pair = jnp.stack([own, other])
    return lax.all_gather(pair, AXES, axis=0, axis_index_groups=Z_CORE_GROUPS)


def local(qkv_txt, qkv_img, dy_txt, dy_img, wv_txt, sc_txt, wv_img, sc_img):
    fsdp, sp = lax.axis_index("fsdp"), lax.axis_index("sp")
    core, x_lo, z = fsdp % 2, fsdp // 32, (fsdp // 2) % 16
    place = jnp.stack(slots(sp) + [core, x_lo]).astype(jnp.int32)

    weights = dequant(wv_txt, sc_txt, wv_img, sc_img)
    other = send(weights, SWAP_X_LO)
    own = jnp.concatenate([dy_txt[0], dy_img[0]], axis=0)
    other, own = lax.optimization_barrier((other, own))
    w = gather_weights(weights, other)
    by_y = {k: send(own, FROM_Y[k]) for k in (1, 3)}
    across = send(own, SWAP_X_HI)

    x = jnp.concatenate(
        [qkv_txt[0].reshape(3, TXT, SP, COLS), qkv_img[0].reshape(3, IMG, SP, COLS)], axis=1
    ).transpose(2, 0, 1, 3)
    by_y[1], x = lax.optimization_barrier((by_y[1], x))
    x = lax.all_to_all(x, "sp", 0, 0, tiled=True)
    att, probs = forward(x)

    far = jnp.stack(
        [send(by_y[1][:, :HALF], FROM_Y[1]), send(by_y[3][:, HALF:], FROM_Y[3])]
    )
    pieces = [own, by_y[1], far, by_y[3]] + [
        across,
        send(across, FROM_Y[1]),
        send(far, SWAP_X_HI),
        send(across, FROM_Y[3]),
    ]
    keep, give = weight_term(place, pieces, att)

    total = plus(keep, send(give, SWAP_CORE)).astype(jnp.bfloat16)
    total, att = lax.optimization_barrier((total, att))
    quads = lax.all_to_all(total, AXES, 0, 0, axis_index_groups=NEAR_GROUPS, tiled=True)
    back = backward(place, pieces, w, x, probs, att)
    back, quads = lax.optimization_barrier((back, quads))
    quads = jnp.sum(quads.astype(jnp.float32), axis=0).astype(jnp.bfloat16)
    back = lax.all_to_all(back, "sp", 0, 0, tiled=True)

    half, row = z // 8, (z // 4) % 2
    quads = quads.reshape(2, 2, ROWS, COLS)
    give = lax.dynamic_index_in_dim(quads, 1 - half, 0, keepdims=False)
    keep = lax.dynamic_index_in_dim(quads, half, 0, keepdims=False)
    pair = plus(keep, send(give, SWAP_Z[8]))
    give = lax.dynamic_index_in_dim(pair, 1 - row, 0, keepdims=False).astype(jnp.bfloat16)
    last = send(give, SWAP_Z[4])
    outs, last = lax.optimization_barrier((spread(back), last))
    keep = lax.dynamic_index_in_dim(pair, row, 0, keepdims=False)
    return (*outs, plus(keep, last) * (1.0 / 64))


def solution(mesh):
    placed = (
        P("fsdp", None, "sp", None),
        P("fsdp", None, "sp", None),
        P("fsdp", "sp", None),
        P("fsdp", "sp", None),
        P("fsdp", "sp"),
        P("fsdp", "sp"),
        P("fsdp", "sp"),
        P("fsdp", "sp"),
    )
    return jax.shard_map(
        local,
        mesh=mesh,
        in_specs=placed,
        out_specs=(P("fsdp", None, "sp", None), P("fsdp", None, "sp", None), P("fsdp", "sp")),
        check_vma=False,
    )
```

```python
import functools
import math

import jax
import jax.numpy as jnp
from jax import lax
from jax.experimental import pallas as pl
from jax.experimental.pallas import tpu as pltpu
from jax.sharding import PartitionSpec as P

HD = 128
SP = 8
TXT = 32
IMG = 96
TOK = TXT + IMG
ALL_TXT = SP * TXT
ALL_IMG = SP * IMG
LENGTH = SP * TOK
COLS = 256
D = 3072
HALF = D // 2
ROWS = 48
HEADS = COLS // HD
CHUNK = 256
FACTOR = 1.0 / math.sqrt(HD)
LOG2E = 1.4426950408889634
SCALE2 = FACTOR * LOG2E
AXES = ("fsdp", "sp")
VMEM_LIMIT = 48 * 1024 * 1024
LIGHT = pl.CostEstimate(flops=1000, bytes_accessed=1000, transcendentals=0)


def number(x_lo, z, core, y, x_hi):
    return ((x_lo * 16 + z) * 2 + core) * SP + y * 2 + x_hi


def every():
    return [
        (x_lo, z, core, y, x_hi)
        for x_lo in range(2)
        for z in range(16)
        for core in range(2)
        for y in range(4)
        for x_hi in range(2)
    ]


def route(target):
    return [(number(*d), number(*target(*d))) for d in every()]


SWAP_CORE = route(lambda x_lo, z, core, y, x_hi: (x_lo, z, 1 - core, y, x_hi))
SWAP_X_LO = route(lambda x_lo, z, core, y, x_hi: (1 - x_lo, z, core, y, x_hi))
SWAP_X_HI = route(lambda x_lo, z, core, y, x_hi: (x_lo, z, core, y, 1 - x_hi))
FROM_Y = {
    k: route(lambda x_lo, z, core, y, x_hi, k=k: (x_lo, z, core, (y - k) % 4, x_hi))
    for k in (1, 3)
}
SWAP_Z = {
    k: route(lambda x_lo, z, core, y, x_hi, k=k: (x_lo, z ^ k, core, y, x_hi)) for k in (4, 8)
}
NEAR_GROUPS = [
    [number(x_lo, 4 * quad + z, core, y, x_hi) for x_lo in range(2) for z in range(4)]
    for quad in range(4)
    for core in range(2)
    for y in range(4)
    for x_hi in range(2)
]
Z_CORE_GROUPS = [
    [number(x_lo, z, core, y, x_hi) for z in range(16) for core in range(2)]
    for x_lo in range(2)
    for y in range(4)
    for x_hi in range(2)
]


def send(x, pairs):
    return lax.ppermute(x, AXES, pairs)


def plus(a, b):
    return a.astype(jnp.float32) + b.astype(jnp.float32)


def dot(a, b):
    return jnp.dot(a, b, preferred_element_type=jnp.float32)


def dot_last(a, b):
    return lax.dot_general(a, b, (((1,), (1,)), ((), ())), preferred_element_type=jnp.float32)


def transposed(x):
    return x.astype(jnp.float32).T


def load_qkv(x_ref, joint, sems):
    copies = []
    for r in range(SP):
        copies.append(
            pltpu.make_async_copy(
                x_ref.at[r, :, pl.ds(0, TXT), :],
                joint.at[:, pl.ds(r * TXT, TXT), :],
                sems.at[2 * r],
            )
        )
        copies.append(
            pltpu.make_async_copy(
                x_ref.at[r, :, pl.ds(TXT, IMG), :],
                joint.at[:, pl.ds(ALL_TXT + r * IMG, IMG), :],
                sems.at[2 * r + 1],
            )
        )
    for copy in copies:
        copy.start()
    return copies


def forward_kernel(x_ref, att_ref, probs_ref, joint, sems):
    for copy in load_qkv(x_ref, joint, sems):
        copy.wait()
    for head in range(HEADS):
        window = slice(head * HD, (head + 1) * HD)
        keys = joint[1, :, window]
        values_t = transposed(joint[2, :, window]).astype(jnp.bfloat16)
        for chunk in range(LENGTH // CHUNK):
            rows = slice(chunk * CHUNK, (chunk + 1) * CHUNK)
            scores = dot_last(keys, joint[0, rows, window])
            highest = jnp.max(scores, axis=0, keepdims=True)
            weights = jnp.exp2((scores - highest) * SCALE2)
            share = 1.0 / jnp.sum(weights, axis=0, keepdims=True)
            probs = (weights * share).astype(jnp.bfloat16)
            probs_ref[head, :, rows] = probs
            att_ref[rows, window] = dot(values_t, probs).T.astype(jnp.bfloat16)


def forward(x):
    return pl.pallas_call(
        forward_kernel,
        out_shape=(
            jax.ShapeDtypeStruct((LENGTH, COLS), jnp.bfloat16),
            jax.ShapeDtypeStruct((HEADS, LENGTH, LENGTH), jnp.bfloat16),
        ),
        in_specs=[pl.BlockSpec(memory_space=pl.ANY)],
        out_specs=(
            pl.BlockSpec(memory_space=pltpu.VMEM),
            pl.BlockSpec(memory_space=pltpu.VMEM),
        ),
        scratch_shapes=[
            pltpu.VMEM((3, LENGTH, COLS), jnp.bfloat16),
            pltpu.SemaphoreType.DMA((2 * SP,)),
        ],
        compiler_params=pltpu.CompilerParams(vmem_limit_bytes=VMEM_LIMIT),
        cost_estimate=LIGHT,
        name="attention_forward",
    )(x)


def slots(sp):
    y, x_hi = sp // 2, sp % 2
    return [((y + k) % 4) * 2 + x_hi for k in range(4)] + [
        ((y + k) % 4) * 2 + 1 - x_hi for k in range(4)
    ]


def load_dy(place_ref, pieces, text, image, sems):
    copies = []
    for target, row, size in [(image, TXT, IMG)] + ([(text, 0, TXT)] if text is not None else []):
        for n, piece in enumerate(pieces):
            rows = pl.ds(pl.multiple_of(place_ref[n] * size, TXT), size)
            if n % 4 == 2:
                ends = [
                    (piece.at[half, pl.ds(row, size), :], target.at[rows, pl.ds(half * HALF, HALF)])
                    for half in range(2)
                ]
            else:
                ends = [(piece.at[pl.ds(row, size), :], target.at[rows, :])]
            for source, place in ends:
                copies.append(pltpu.make_async_copy(source, place, sems.at[len(copies)]))
    for copy in copies:
        copy.start()
    return copies


BAND = 8 * 2 * ROWS


def term_kernel(place_ref, *refs):
    pieces, (att_ref, keep_ref, give_ref, image, sems) = refs[:SP], refs[SP:]
    copies = load_dy(place_ref, pieces, None, image, sems)
    att_t = transposed(att_ref[ALL_TXT:, :]).astype(jnp.bfloat16)
    for copy in copies:
        copy.wait()
    core = place_ref[SP]
    for band in range(D // BAND):
        term = dot(att_t, image[:, band * BAND : (band + 1) * BAND]).T.astype(jnp.bfloat16)
        for j in range(8):
            z = (band % 2) * 8 + j
            low = term[(2 * j) * ROWS : (2 * j + 1) * ROWS]
            high = term[(2 * j + 1) * ROWS : (2 * j + 2) * ROWS]
            keep_ref[4 * (band // 2) + z % 4, z // 4] = jnp.where(core == 0, low, high)
            give_ref[4 * (band // 2) + z % 4, z // 4] = jnp.where(core == 0, high, low)


def weight_term(place, pieces, att):
    half = jax.ShapeDtypeStruct((8, 4, ROWS, COLS), jnp.bfloat16)
    return pl.pallas_call(
        term_kernel,
        out_shape=(half, half),
        in_specs=[pl.BlockSpec(memory_space=pltpu.SMEM)]
        + [pl.BlockSpec(memory_space=pl.ANY)] * SP
        + [pl.BlockSpec(memory_space=pltpu.VMEM)],
        out_specs=(
            pl.BlockSpec(memory_space=pltpu.VMEM),
            pl.BlockSpec(memory_space=pltpu.VMEM),
        ),
        scratch_shapes=[
            pltpu.VMEM((SP * IMG, D), jnp.bfloat16),
            pltpu.SemaphoreType.DMA((SP + 2,)),
        ],
        compiler_params=pltpu.CompilerParams(vmem_limit_bytes=VMEM_LIMIT),
        cost_estimate=LIGHT,
        name="weight_term",
    )(place, *pieces, att)


def head_backward(window, joint, grad, att, probs, slopes, out_ref, out_window):
    keys, values = joint[1, :, window], joint[2, :, window]
    keys_t = transposed(keys).astype(jnp.bfloat16)

    def put(member, first, block):
        for r in range(SP):
            lo, hi = r * TXT - first, (r + 1) * TXT - first
            if 0 <= lo < block.shape[0]:
                out_ref[r, member, :TXT, out_window] = block[lo:hi]
            lo, hi = ALL_TXT + r * IMG - first, ALL_TXT + (r + 1) * IMG - first
            start, stop = max(lo, 0), min(hi, block.shape[0])
            if start < stop:
                rows = slice(TXT + start - lo, TXT + stop - lo)
                out_ref[r, member, rows, out_window] = block[start:stop]

    for chunk in range(LENGTH // CHUNK):
        rows = slice(chunk * CHUNK, (chunk + 1) * CHUNK)
        out_grad = grad[rows]
        product = out_grad.astype(jnp.float32) * att[rows].astype(jnp.float32)
        delta = jnp.sum(product.T, axis=0, keepdims=True)
        change = dot_last(values, out_grad) - delta
        slope = (probs[:, rows].astype(jnp.float32) * change).astype(jnp.bfloat16)
        slopes[:, rows] = slope
        put(0, chunk * CHUNK, (dot(keys_t, slope) * FACTOR).T.astype(jnp.bfloat16))
    put(1, 0, (dot(slopes[...], joint[0, :, window]) * FACTOR).astype(jnp.bfloat16))
    put(2, 0, dot(probs[...], grad[...]).astype(jnp.bfloat16))


def backward_kernel(place_ref, *refs):
    pieces, rest = refs[:SP], refs[SP:]
    w_ref, x_ref, probs_ref, att, out_ref = rest[:5]
    grad, text, image, weight, joint, probs, slopes, sems, dy_sems, qkv_sems = rest[5:]
    x_lo = place_ref[SP + 1]
    copies = [
        pltpu.make_async_copy(
            w_ref.at[:, n, stream],
            weight.at[stream, (x_lo + n) % 2],
            sems.at[2 * stream + n],
        )
        for stream in range(2)
        for n in range(2)
    ]
    for copy in copies[2:]:
        copy.start()
    dy_copies = load_dy(place_ref, pieces, text, image, dy_sems)
    for copy in copies[:2]:
        copy.start()
    late = load_qkv(x_ref, joint, qkv_sems)
    probs_copies = [
        pltpu.make_async_copy(probs_ref.at[head], probs.at[head], sems.at[4 + head])
        for head in range(HEADS)
    ]
    for copy in probs_copies:
        copy.start()
    for copy in copies[2:] + dy_copies[: SP + 2]:
        copy.wait()
    grad[ALL_TXT:, :] = dot(image[...], weight[1].reshape(D, COLS)).astype(jnp.bfloat16)
    for copy in copies[:2] + dy_copies[SP + 2 :]:
        copy.wait()
    grad[:ALL_TXT, :] = dot(text[...], weight[0].reshape(D, COLS)).astype(jnp.bfloat16)
    for copy in late:
        copy.wait()
    for head in range(HEADS):
        window = slice(head * HD, (head + 1) * HD)
        probs_copies[head].wait()
        head_backward(
            window, joint, grad[:, window], att[:, window], probs[head], slopes, out_ref, window
        )


ANY = pl.BlockSpec(memory_space=pl.ANY)
VMEM = pl.BlockSpec(memory_space=pltpu.VMEM)


def backward(place, pieces, w, x, probs, att):
    return pl.pallas_call(
        backward_kernel,
        out_shape=jax.ShapeDtypeStruct((SP, 3, TOK, COLS), jnp.bfloat16),
        in_specs=[pl.BlockSpec(memory_space=pltpu.SMEM)] + [ANY] * (SP + 3) + [VMEM],
        out_specs=VMEM,
        scratch_shapes=[
            pltpu.VMEM((LENGTH, COLS), jnp.bfloat16),
            pltpu.VMEM((ALL_TXT, D), jnp.bfloat16),
            pltpu.VMEM((ALL_IMG, D), jnp.bfloat16),
            pltpu.VMEM((2, 2, 32, ROWS, COLS), jnp.bfloat16),
            pltpu.VMEM((3, LENGTH, COLS), jnp.bfloat16),
            pltpu.VMEM((HEADS, LENGTH, LENGTH), jnp.bfloat16),
            pltpu.VMEM((LENGTH, LENGTH), jnp.bfloat16),
            pltpu.SemaphoreType.DMA((6,)),
            pltpu.SemaphoreType.DMA((2 * SP + 4,)),
            pltpu.SemaphoreType.DMA((2 * SP,)),
        ],
        compiler_params=pltpu.CompilerParams(vmem_limit_bytes=VMEM_LIMIT),
        cost_estimate=pl.CostEstimate(
            flops=HEADS * 8 * LENGTH * LENGTH * HD + 2 * LENGTH * D * COLS,
            bytes_accessed=LENGTH * D * 2 + 2 * D * COLS * 2 + 24 * LENGTH * LENGTH,
            transcendentals=0,
        ),
        name="project_and_backward",
    )(place, *pieces, w, x, probs, att)


def spread_kernel(back_ref, txt_ref, img_ref):
    for r in range(SP):
        columns = slice(r * COLS, (r + 1) * COLS)
        txt_ref[0, :, :, columns] = back_ref[r, :, :TXT, :]
        img_ref[0, :, :, columns] = back_ref[r, :, TXT:, :]


def spread(back):
    return pl.pallas_call(
        spread_kernel,
        out_shape=(
            jax.ShapeDtypeStruct((1, 3, TXT, SP * COLS), jnp.bfloat16),
            jax.ShapeDtypeStruct((1, 3, IMG, SP * COLS), jnp.bfloat16),
        ),
        in_specs=[VMEM],
        out_specs=(VMEM, VMEM),
        compiler_params=pltpu.CompilerParams(vmem_limit_bytes=VMEM_LIMIT),
        cost_estimate=LIGHT,
        name="spread_features",
    )(back)


def dequant_kernel(txt_ref, txt_scales, img_ref, img_scales, out_ref):
    for stream, (values, scales) in enumerate(((txt_ref, txt_scales), (img_ref, img_scales))):
        by_row = scales[...].T
        for head in range(HEADS):
            window = slice(head * HD, (head + 1) * HD)
            scaled = values[:, window].astype(jnp.float32) * by_row[:, head : head + 1]
            out_ref[stream, :, window] = scaled.astype(jnp.bfloat16)


def dequant(wv_txt, sc_txt, wv_img, sc_img):
    return pl.pallas_call(
        dequant_kernel,
        out_shape=jax.ShapeDtypeStruct((2, ROWS, COLS), jnp.bfloat16),
        in_specs=[VMEM] * 4,
        out_specs=VMEM,
        cost_estimate=LIGHT,
        name="dequantize",
    )(wv_txt, sc_txt.T, wv_img, sc_img.T)


def gather_weights(own, other):
    pair = jnp.stack([own, other])
    return lax.all_gather(pair, AXES, axis=0, axis_index_groups=Z_CORE_GROUPS)


def local(qkv_txt, qkv_img, dy_txt, dy_img, wv_txt, sc_txt, wv_img, sc_img):
    fsdp, sp = lax.axis_index("fsdp"), lax.axis_index("sp")
    core, x_lo, z = fsdp % 2, fsdp // 32, (fsdp // 2) % 16
    place = jnp.stack(slots(sp) + [core, x_lo]).astype(jnp.int32)

    weights = dequant(wv_txt, sc_txt, wv_img, sc_img)
    other = send(weights, SWAP_X_LO)
    own = jnp.concatenate([dy_txt[0], dy_img[0]], axis=0)
    other, own = lax.optimization_barrier((other, own))
    w = gather_weights(weights, other)
    by_y = {k: send(own, FROM_Y[k]) for k in (1, 3)}
    across = send(own, SWAP_X_HI)

    x = jnp.concatenate(
        [qkv_txt[0].reshape(3, TXT, SP, COLS), qkv_img[0].reshape(3, IMG, SP, COLS)], axis=1
    ).transpose(2, 0, 1, 3)
    by_y[1], x = lax.optimization_barrier((by_y[1], x))
    x = lax.all_to_all(x, "sp", 0, 0, tiled=True)
    att, probs = forward(x)

    far = jnp.stack(
        [send(by_y[1][:, :HALF], FROM_Y[1]), send(by_y[3][:, HALF:], FROM_Y[3])]
    )
    far, across = lax.optimization_barrier((far, across))
    pieces = [own, by_y[1], far, by_y[3]] + [
        across,
        send(across, FROM_Y[1]),
        send(far, SWAP_X_HI),
        send(across, FROM_Y[3]),
    ]
    keep, give = weight_term(place, pieces, att)

    total = plus(keep, send(give, SWAP_CORE)).astype(jnp.bfloat16)
    total, att = lax.optimization_barrier((total, att))
    quads = lax.all_to_all(total, AXES, 0, 0, axis_index_groups=NEAR_GROUPS, tiled=True)
    back = backward(place, pieces, w, x, probs, att)
    back, quads = lax.optimization_barrier((back, quads))
    quads = jnp.sum(quads.astype(jnp.float32), axis=0).astype(jnp.bfloat16)
    back = lax.all_to_all(back, "sp", 0, 0, tiled=True)

    half, row = z // 8, (z // 4) % 2
    quads = quads.reshape(2, 2, ROWS, COLS)
    give = lax.dynamic_index_in_dim(quads, 1 - half, 0, keepdims=False)
    keep = lax.dynamic_index_in_dim(quads, half, 0, keepdims=False)
    pair = plus(keep, send(give, SWAP_Z[8]))
    give = lax.dynamic_index_in_dim(pair, 1 - row, 0, keepdims=False).astype(jnp.bfloat16)
    last = send(give, SWAP_Z[4])
    outs, last = lax.optimization_barrier((spread(back), last))
    keep = lax.dynamic_index_in_dim(pair, row, 0, keepdims=False)
    return (*outs, plus(keep, last) * (1.0 / 64))


def solution(mesh):
    placed = (
        P("fsdp", None, "sp", None),
        P("fsdp", None, "sp", None),
        P("fsdp", "sp", None),
        P("fsdp", "sp", None),
        P("fsdp", "sp"),
        P("fsdp", "sp"),
        P("fsdp", "sp"),
        P("fsdp", "sp"),
    )
    return jax.shard_map(
        local,
        mesh=mesh,
        in_specs=placed,
        out_specs=(P("fsdp", None, "sp", None), P("fsdp", None, "sp", None), P("fsdp", "sp")),
        check_vma=False,
    )
```
